128 devices in a mesh: ctx: 32 (over y, x_lo, z), dp: 4 (over x_hi, core).
Axes of the slice: x: 4 (x_hi: 2, x_lo: 2; x = x_hi * 2 + x_lo), y: 4, z: 4, core: 2. Of those that a mesh axis runs over, the one named last changes fastest.
Arguments:
- query_raw: bfloat16 [4, 16384, 2048], P('dp', 'ctx'), may hold values from -6 to 6
- key_raw: bfloat16 [4, 16384, 1024], P('dp', 'ctx'), may hold values from -6 to 6
- values: bfloat16 [4, 16384, 1024], P('dp', 'ctx'), may hold values from -6 to 6
- out_grad: bfloat16 [4, 16384, 2048], P('dp', 'ctx'), may hold values from -36 to 36
- query_scale: float32 [128], replicated, may hold values from 0.5 to 6
- key_scale: float32 [128], replicated, may hold values from 0.5 to 6
- block_doc: int32 [4, 16], P('dp'), may hold values from 0 to 14, as said below
- doc_end: int32 [4, 16], P('dp'), may hold values from 0 to 16384, as said below
Outputs:
- attended: bfloat16 [4, 16384, 2048], P('dp', 'ctx')
- query_grad: bfloat16 [4, 16384, 2048], P('dp', 'ctx')
- key_grad: bfloat16 [4, 16384, 1024], P('dp', 'ctx')
- value_grad: bfloat16 [4, 16384, 1024], P('dp', 'ctx')
- query_scale_grad: float32 [128], replicated
- key_scale_grad: float32 [128], replicated
The draws below stay inside these ranges and needn't reach their ends.
Inputs may be any that keep to these rules, and one draw needn't show every extreme that they name: `block_doc`: along each sequence the document id is 0 in the first block and rises by 0 or 1 from block to block; documents start at multiples of 1024. In every draw one sequence starts a new document at every block but the second. `doc_end`: entry d is one past the last real token of document d; the rest of the document's last block is padding; the last document of a sequence ends at 16384; unused entries are 0.
All inputs are finite; a program needn't handle non-finite values.
Results may differ from the reference program's by a relative error of at most 0.0035.
The reference program's roundings to bfloat16 on the way (of `query_norm`, `key_norm`, `weights` and `score_grad`) count: a program that leaves them out, or rounds other values in their place, can miss the bound.
Values may be sent and summed in bfloat16 or wider, within the bound.
A program may use at most 192 MiB of HBM per device.

```python
import jax
import jax.numpy as jnp
from jax import lax

HEADS = 16
KV_HEADS = 8
HD = 128
WINDOW = 1024
BLOCK = 1024
TOK_DEV = 512
SEQS = 4
LENGTH = 16384
BLOCKS = 16


def raw_pair(key):
    query_shape = (SEQS, LENGTH, HEADS * HD)
    key_shape = (SEQS, LENGTH, KV_HEADS * HD)
    query_draw = jnp.clip(jax.random.normal(jax.random.fold_in(key, 11), query_shape, jnp.float32), -6.0, 6.0)
    key_draw = jnp.clip(jax.random.normal(jax.random.fold_in(key, 12), key_shape, jnp.float32), -6.0, 6.0)
    return (query_draw, key_draw)


def draw_query_raw(key, part):
    return raw_pair(key)[0].astype(jnp.bfloat16)


def draw_key_raw(key, part):
    return raw_pair(key)[1].astype(jnp.bfloat16)


def draw_out_grad(key, part):
    grad_shape = (SEQS, LENGTH, HEADS * HD)
    ramp = lax.broadcasted_iota(jnp.float32, (1, LENGTH, 1), 1) / (LENGTH - 1)
    normal_part = jnp.clip(jax.random.normal(jax.random.fold_in(key, 41), grad_shape, jnp.float32), -4.0, 4.0)
    return (normal_part * (1.0 + 2.0 * ramp)).astype(jnp.bfloat16)


def scale_draw(key):
    return 0.5 * jnp.power(4.0, jax.random.uniform(key, (HD,), jnp.float32))


def draw_query_scale(key, part):
    return scale_draw(jax.random.fold_in(key, 31))


def draw_key_scale(key, part):
    return scale_draw(jax.random.fold_in(key, 32))


def doc_layout(key):
    column = lax.broadcasted_iota(jnp.int32, (SEQS, BLOCKS), 1)
    seq_place = lax.broadcasted_iota(jnp.int32, (SEQS, BLOCKS), 0)
    chosen_seq = jax.random.randint(jax.random.fold_in(key, 23), (), 0, SEQS)
    coin_toss = jax.random.randint(jax.random.fold_in(key, 21), (SEQS, BLOCKS), 0, 3)
    every_block = (seq_place == chosen_seq) & (column != 1)
    starts = (column == 0) | (coin_toss == 0) & (column != 1) | every_block
    doc_ids = (jnp.cumsum(starts.astype(jnp.int32), axis=1) - 1).astype(jnp.int32)
    following = jnp.concatenate([starts[:, 1:], jnp.ones((SEQS, 1), jnp.bool_)], axis=1)
    filled = jax.random.randint(jax.random.fold_in(key, 22), (SEQS, BLOCKS), 64, BLOCK + 1)
    filled = jnp.where(column == BLOCKS - 1, BLOCK, filled)
    ends_at = column * BLOCK + filled
    doc_slots = lax.broadcasted_iota(jnp.int32, (SEQS, BLOCKS, BLOCKS), 2)
    last_hits = (doc_ids[:, :, None] == doc_slots) & following[:, :, None]
    doc_table = jnp.max(jnp.where(last_hits, ends_at[:, :, None], 0), axis=1).astype(jnp.int32)
    return (doc_ids, doc_table)


def draw_block_doc(key, part):
    return doc_layout(key)[0]


def draw_doc_end(key, part):
    return doc_layout(key)[1]


def level_of(own_key, dims, cuts, least, largest):
    level, own = 1.0, jax.random.fold_in(own_key, 6)
    for axis_at, parts in cuts:
        draws = jnp.exp(jax.random.uniform(jax.random.fold_in(own, axis_at), (parts,), jnp.float32, least / len(cuts), largest / len(cuts)))
        level = level * jnp.repeat(draws, dims[axis_at] // parts).reshape([-1 if axis == axis_at else 1 for axis in range(len(dims))])
    return level


def bell_draw(rng, extent, scale, limit, cuts=(), kind=jnp.bfloat16):
    factor_of = level_of(rng, extent, cuts, -0.22, 0.18) if cuts else 1.0
    result = jax.random.normal(rng, extent, jnp.float32) * scale * factor_of
    return jnp.minimum(jnp.maximum(result, -limit), limit).astype(kind)


def setup_inputs(seed: int = 0) -> dict:
    seeds = jax.random.split(jax.random.key(seed), 9)
    return {
        "query_raw": draw_query_raw(jax.random.fold_in(seeds[8], 71), 0),
        "key_raw": draw_key_raw(jax.random.fold_in(seeds[8], 71), 0),
        "values": bell_draw(seeds[2], (SEQS, LENGTH, KV_HEADS * HD), 1.0, 6.0, ((0, 4), (1, 32))),
        "out_grad": draw_out_grad(jax.random.fold_in(seeds[8], 71), 0),
        "query_scale": draw_query_scale(jax.random.fold_in(seeds[8], 71), 0),
        "key_scale": draw_key_scale(jax.random.fold_in(seeds[8], 71), 0),
        "block_doc": draw_block_doc(jax.random.fold_in(seeds[8], 71), 0),
        "doc_end": draw_doc_end(jax.random.fold_in(seeds[8], 71), 0),
    }


score_scale = 168.0 ** (-0.5)
norm_eps = 1e-06

def head_norm(inputs, scales):
    mean_square = lax.optimization_barrier(jnp.mean(inputs * inputs, axis=-1, keepdims=True))
    return inputs * lax.rsqrt(mean_square + norm_eps) * scales

def lookup(entries, wanted):
    places = lax.iota(jnp.int32, entries.shape[0])
    return jnp.sum(jnp.where(places == wanted, entries, 0)).astype(jnp.int32)

def shard_facts(query_shard, offset, doc_row, end_row, shard_rows, shards):
    source = query_shard - offset
    query_doc = lookup(doc_row, query_shard * shard_rows // BLOCK)
    source_doc = lookup(doc_row, source * shard_rows // BLOCK)
    live_flag = (source >= 0) & (query_shard < shards) & (source_doc == query_doc)
    return (live_flag, source * shard_rows, lookup(end_row, source_doc))

def tile_mask(offset, live_flag, key_start, key_limit, tile_rows):
    query_place = lax.broadcasted_iota(jnp.int32, (tile_rows, tile_rows), 0)
    key_place = lax.broadcasted_iota(jnp.int32, (tile_rows, tile_rows), 1)
    distance = offset * tile_rows + query_place - key_place
    inside = (distance >= 0) & (distance < WINDOW)
    usable = key_start + key_place < key_limit
    return inside & usable & live_flag

def rounded_earlier(part):
    earlier = lax.optimization_barrier(part[:2 * TOK_DEV].astype(jnp.bfloat16)).astype(jnp.float32)
    return jnp.concatenate([earlier, part[2 * TOK_DEV:]], axis=0)

def one_sequence(query_rows, key_rows, value_rows, grad_rows, query_scale, key_scale, doc_row, end_row):
    length = query_rows.shape[0]
    group_size = HEADS // KV_HEADS
    shards = length // TOK_DEV
    query_float = query_rows.astype(jnp.float32).reshape(length, HEADS, HD)
    key_float = key_rows.astype(jnp.float32).reshape(length, KV_HEADS, HD)
    query_norm = head_norm(query_float, query_scale).astype(jnp.bfloat16).reshape(length, KV_HEADS, group_size, HD)
    key_norm = head_norm(key_float, key_scale).astype(jnp.bfloat16)
    margin = jnp.zeros((2 * TOK_DEV, KV_HEADS, HD), jnp.bfloat16)
    key_padded = jnp.concatenate([margin, key_norm], axis=0)
    value_padded = jnp.concatenate([margin, value_rows.reshape(length, KV_HEADS, HD)], axis=0)
    grad_heads = grad_rows.reshape(length, KV_HEADS, group_size, HD)

    def block_step(carried, shard_index):
        key_sum, value_sum = carried
        first_row = shard_index * TOK_DEV
        query_block = lax.dynamic_slice_in_dim(query_norm, first_row, TOK_DEV, 0).astype(jnp.float32)
        grad_block = lax.dynamic_slice_in_dim(grad_heads, first_row, TOK_DEV, 0).astype(jnp.float32)
        key_block = lax.dynamic_slice_in_dim(key_padded, first_row, 3 * TOK_DEV, 0).astype(jnp.float32)
        value_block = lax.dynamic_slice_in_dim(value_padded, first_row, 3 * TOK_DEV, 0).astype(jnp.float32)
        mask_list = []
        for offset in (2, 1, 0):
            live_flag, key_start, key_limit = shard_facts(shard_index, offset, doc_row, end_row, TOK_DEV, shards)
            mask_list.append(tile_mask(offset, live_flag, key_start, key_limit, TOK_DEV))
        allowed = jnp.concatenate(mask_list, axis=1)
        scores = jnp.einsum('qhgd,khd->hgqk', query_block, key_block) * score_scale
        scores = jnp.where(allowed, scores, -jnp.inf)
        row_peak = lax.optimization_barrier(jnp.max(scores, axis=-1, keepdims=True))
        log_total = row_peak + jnp.log(lax.optimization_barrier(jnp.sum(jnp.exp(scores - row_peak), axis=-1, keepdims=True)))
        shares = jnp.exp(scores - log_total)
        weights = lax.optimization_barrier(shares.astype(jnp.bfloat16)).astype(jnp.float32)
        attended = jnp.einsum('hgqk,khd->qhgd', weights, value_block).astype(jnp.bfloat16)
        attended_float = lax.optimization_barrier(attended).astype(jnp.float32)
        row_delta = jnp.einsum('qhgd,qhgd->hgq', grad_block, attended_float)[..., None]
        share_grad = jnp.einsum('qhgd,khd->hgqk', grad_block, value_block)
        score_grad = (shares * (share_grad - row_delta) * score_scale).astype(jnp.bfloat16)
        score_grad = lax.optimization_barrier(score_grad).astype(jnp.float32)
        query_part = jnp.einsum('hgqk,khd->qhgd', score_grad, key_block)
        key_part = rounded_earlier(jnp.einsum('hgqk,qhgd->khd', score_grad, query_block))
        value_part = rounded_earlier(jnp.einsum('hgqk,qhgd->khd', weights, grad_block))
        key_sum = lax.dynamic_update_slice_in_dim(key_sum, lax.dynamic_slice_in_dim(key_sum, first_row, 3 * TOK_DEV, 0) + key_part, first_row, 0)
        value_sum = lax.dynamic_update_slice_in_dim(value_sum, lax.dynamic_slice_in_dim(value_sum, first_row, 3 * TOK_DEV, 0) + value_part, first_row, 0)
        return ((key_sum, value_sum), (attended, query_part))
    empty_sums = jnp.zeros((length + 2 * TOK_DEV, KV_HEADS, HD), jnp.float32)
    shard_list = jnp.arange(shards, dtype=jnp.int32)
    (key_sum, value_sum), (attended, query_norm_grad) = lax.scan(block_step, (empty_sums, empty_sums), shard_list)
    attended = attended.reshape(length, HEADS * HD)
    query_norm_grad = query_norm_grad.reshape(length, HEADS, HD)
    normed, query_pull = jax.vjp(head_norm, query_float, query_scale)
    query_grad, query_scale_grad = query_pull(query_norm_grad)
    normed, key_pull = jax.vjp(head_norm, key_float, key_scale)
    key_grad, key_scale_grad = key_pull(key_sum[2 * TOK_DEV:])
    value_grad = value_sum[2 * TOK_DEV:].astype(jnp.bfloat16).reshape(length, KV_HEADS * HD)
    query_grad = query_grad.astype(jnp.bfloat16).reshape(length, HEADS * HD)
    key_grad = key_grad.astype(jnp.bfloat16).reshape(length, KV_HEADS * HD)
    return (attended, query_grad, key_grad, value_grad, query_scale_grad, key_scale_grad)

def reference(query_raw, key_raw, values, out_grad, query_scale, key_scale, block_doc, doc_end):
    results = []
    for seq_index in range(SEQS):
        results.append(one_sequence(query_raw[seq_index], key_raw[seq_index], values[seq_index], out_grad[seq_index], query_scale, key_scale, block_doc[seq_index], doc_end[seq_index]))
    attended = jnp.stack([outcome[0] for outcome in results])
    query_grad = jnp.stack([outcome[1] for outcome in results])
    key_grad = jnp.stack([outcome[2] for outcome in results])
    value_grad = jnp.stack([outcome[3] for outcome in results])
    query_scale_grad = results[0][4]
    key_scale_grad = results[0][5]
    for seq_index in range(1, SEQS):
        query_scale_grad = query_scale_grad + results[seq_index][4]
        key_scale_grad = key_scale_grad + results[seq_index][5]
    return (attended, query_grad, key_grad, value_grad, query_scale_grad, key_scale_grad)
```

```python
import functools

import jax
import jax.numpy as jnp
from jax import lax
from jax.experimental import pallas as pl
from jax.experimental.pallas import tpu as pltpu
from jax.sharding import PartitionSpec as P

WINDOW = 1024
BLOCK = 1024
MESH = pl.DeviceIdType.MESH
F32 = jnp.float32
BF16 = jnp.bfloat16

score_scale = 168.0 ** (-0.5)
LOG2E = 1.4426950408889634
norm_eps = 1e-06
MASKED = -1e30

HD = 128
T = 512
QB = 256
KB = 256
SPAN = WINDOW + QB
VMEM_LIMIT = 48 * 1024 * 1024


def dot(a, b):
    return lax.dot_general(a, b, (((1,), (0,)), ((), ())), preferred_element_type=F32)


def fold_rows(x, op):
    return op(x.reshape(x.shape[0] // 8, 8, x.shape[1]), axis=0)


def kernel(
    heads,
    ctx_size,
    dp_size,
    inner,
    q_hbm,
    k_hbm,
    v_hbm,
    do_hbm,
    qs_ref,
    ks_ref,
    doc_ref,
    end_ref,
    att_hbm,
    dq_hbm,
    dk_hbm,
    dv_hbm,
    qsg_ref,
    ksg_ref,
    qbuf,
    dobuf,
    kvbuf,
    attbuf,
    dqbuf,
    dkvout,
    kn,
    knt,
    vt,
    khat,
    qst,
    s_buf,
    p_buf,
    ds_buf,
    dkacc,
    dvacc,
    own,
    g2send,
    g1buf,
    g2recv,
    g1recv,
    qsacc,
    ksacc,
    ar1,
    ar2,
    ar3,
    load_sem,
    store_sem,
    a_send,
    a_recv,
    r_send,
    r_recv,
    g2_send,
    g2_recv,
    g1_send,
    g1_recv,
    ar_send,
    ar_recv,
):
    me = lax.axis_index("ctx")
    dp = lax.axis_index("dp")
    nxt = lax.rem(me + 1, ctx_size)
    prv = lax.rem(me + ctx_size - 1, ctx_size)
    outer = ctx_size // inner
    me_in = lax.rem(me, inner)
    me_out = me // inner

    def load_copies(h):
        wide = pl.ds(pl.multiple_of(h * 2 * HD, 2 * HD), 2 * HD)
        narrow = pl.ds(pl.multiple_of(h * HD, HD), HD)
        return (
            pltpu.make_async_copy(k_hbm.at[:, narrow], kvbuf.at[h, 0, pl.ds(2 * T, T)], load_sem.at[h, 0]),
            pltpu.make_async_copy(v_hbm.at[:, narrow], kvbuf.at[h, 1, pl.ds(2 * T, T)], load_sem.at[h, 1]),
            pltpu.make_async_copy(q_hbm.at[:, wide], qbuf.at[h], load_sem.at[h, 2]),
            pltpu.make_async_copy(do_hbm.at[:, wide], dobuf.at[h], load_sem.at[h, 3]),
        )

    def query_stores(h):
        wide = pl.ds(pl.multiple_of(h * 2 * HD, 2 * HD), 2 * HD)
        return (
            pltpu.make_async_copy(attbuf.at[h], att_hbm.at[:, wide], store_sem.at[h, 0]),
            pltpu.make_async_copy(dqbuf.at[h], dq_hbm.at[:, wide], store_sem.at[h, 1]),
        )

    def key_stores(h):
        narrow = pl.ds(pl.multiple_of(h * HD, HD), HD)
        return (
            pltpu.make_async_copy(dkvout.at[h, 0], dk_hbm.at[:, narrow], store_sem.at[h, 2]),
            pltpu.make_async_copy(dkvout.at[h, 1], dv_hbm.at[:, narrow], store_sem.at[h, 3]),
        )

    def remote(src, dst, send, recv, device):
        return pltpu.make_async_remote_copy(
            src_ref=src, dst_ref=dst, send_sem=send, recv_sem=recv, device_id=device, device_id_type=MESH
        )

    def halo_near(h):
        narrow = pl.ds(pl.multiple_of(h * HD, HD), HD)
        near = pl.ds(T, T)
        return (
            remote(k_hbm.at[:, narrow], kvbuf.at[h, 0, near], a_send.at[h, 0], a_recv.at[h, 0], {"ctx": nxt}),
            remote(v_hbm.at[:, narrow], kvbuf.at[h, 1, near], a_send.at[h, 1], a_recv.at[h, 1], {"ctx": nxt}),
        )

    def halo_far(h):
        return remote(
            kvbuf.at[h, :, pl.ds(T, T)], kvbuf.at[h, :, pl.ds(0, T)], r_send.at[h], r_recv.at[h], {"ctx": nxt}
        )

    def grad_far(h):
        return remote(g2send.at[h], g2recv.at[h], g2_send.at[h], g2_recv.at[h], {"ctx": prv})

    def grad_near(h):
        return remote(g1buf.at[h], g1recv.at[h], g1_send.at[h], g1_recv.at[h], {"ctx": prv})

    def partners(stage):
        if stage == 0:
            return [{"dp": lax.rem(dp + d, dp_size)} for d in range(1, dp_size)]
        if stage == 1:
            return [{"ctx": me_out * inner + lax.rem(me_in + d, inner)} for d in range(1, inner)]
        return [{"ctx": lax.rem(me_out + d, outer) * inner + me_in} for d in range(1, outer)]

    stage_slot = (dp, me_in, me_out)
    stage_buf = (ar1, ar2, ar3)
    stage_base = (0, dp_size - 1, dp_size + inner - 2)

    def stage_copies(stage):
        slot = stage_buf[stage].at[stage_slot[stage]]
        base = stage_base[stage]
        return [
            remote(slot, slot, ar_send.at[base + d], ar_recv.at[base + d], device)
            for d, device in enumerate(partners(stage))
        ]

    def stage_start(stage, value):
        stage_buf[stage][stage_slot[stage]] = value
        for copy in stage_copies(stage):
            copy.start()

    def stage_sum(stage):
        for copy in stage_copies(stage):
            copy.wait()
        total = stage_buf[stage][0]
        for slot in range(1, stage_buf[stage].shape[0]):
            total = total + stage_buf[stage][slot]
        return total

    def start_loads(h, carry):
        for copy in load_copies(h):
            copy.start()
        return carry

    lax.fori_loop(0, heads, start_loads, 0)

    barrier = pltpu.get_barrier_semaphore()
    greeted = [{"ctx": nxt}, {"ctx": prv}] + partners(0) + partners(1) + partners(2)
    for device in greeted:
        pl.semaphore_signal(barrier, inc=1, device_id=device, device_id_type=MESH)
    pl.semaphore_wait(barrier, len(greeted))

    def start_halo(h):
        for copy in halo_near(h):
            copy.start()

    for h in range(min(3, heads)):
        start_halo(h)

    qrow = qs_ref[...]
    krow = ks_ref[...]
    half = jnp.transpose(jnp.broadcast_to(qrow, (HD, HD)))
    qst[...] = jnp.concatenate([half, half], axis=1)
    qsacc[...] = jnp.zeros_like(qsacc)
    ksacc[...] = jnp.zeros_like(ksacc)

    block = me * T // BLOCK
    doc = doc_ref[0, block]
    before = doc_ref[0, jnp.maximum(block - 1, 0)]
    same = (block > 0) & (doc == before)
    into = me * T - block * BLOCK
    first = jnp.where(same, 0, 2 * T - into)
    limit = end_ref[0, doc] - (me - 2) * T

    def relay(h):
        for copy in halo_near(h):
            copy.wait_recv()
        halo_far(h).start()

    relay(0)

    def prepare(h):
        def prep_block(b, carry):
            rows = pl.ds(pl.multiple_of(b * KB, KB), KB)
            x = kvbuf[h, 0, rows, :].astype(F32)
            mean_square = jnp.mean(x * x, axis=1, keepdims=True)
            hat = x * lax.rsqrt(mean_square + norm_eps)
            khat[rows, :] = hat
            normed = (hat * krow).astype(BF16)
            kn[rows, :] = normed
            knt[:, rows] = jnp.transpose(normed)
            vt[:, rows] = jnp.transpose(kvbuf[h, 1, rows, :])
            return carry

        lax.fori_loop(0, 3 * T // KB, prep_block, 0)

    def unit(h, g, j):
        rows = pl.ds(j * QB, QB)
        cols = pl.ds(g * HD, HD)
        k0 = j * QB
        nb = SPAN // KB
        gain = qst[...]
        xt = jnp.transpose(qbuf[h, rows, cols].astype(F32))
        mean_square = jnp.mean(xt * xt, axis=0, keepdims=True)
        r = lax.rsqrt(mean_square + norm_eps)
        xr = xt * r
        qt = (xr * gain).astype(BF16)
        do = dobuf[h, rows, cols]
        dot_t = jnp.transpose(do)
        lane = lax.broadcasted_iota(jnp.int32, (1, QB), 1)
        low = jnp.maximum(first, k0 + 1 + lane)
        high = jnp.minimum(limit, k0 + 1 + WINDOW + lane)
        place = lax.broadcasted_iota(jnp.int32, (KB, QB), 0)
        peak = jnp.full((8, QB), MASKED, F32)
        for b in range(nb):
            keys = kn[k0 + b * KB : k0 + (b + 1) * KB, :]
            s = dot(keys, qt)
            spot = place + (k0 + b * KB)
            s = jnp.where((spot >= low) & (spot < high), s, MASKED)
            s_buf[b * KB : (b + 1) * KB, :] = s
            peak = jnp.maximum(peak, fold_rows(s, jnp.max))
        peak = jnp.max(peak, axis=0, keepdims=True)
        total = jnp.zeros((8, QB), F32)
        for b in range(nb):
            e = jnp.exp2((s_buf[b * KB : (b + 1) * KB, :] - peak) * (score_scale * LOG2E))
            s_buf[b * KB : (b + 1) * KB, :] = e
            total = total + fold_rows(e, jnp.sum)
        inverse = 1.0 / jnp.sum(total, axis=0, keepdims=True)
        for b in range(nb):
            p_buf[b * KB : (b + 1) * KB, :] = (s_buf[b * KB : (b + 1) * KB, :] * inverse).astype(BF16)
        o = dot(vt[:, k0 : k0 + SPAN], p_buf[...]).astype(BF16)
        attbuf[h, rows, cols] = jnp.transpose(o)
        delta = jnp.sum(dot_t.astype(F32) * o.astype(F32), axis=0, keepdims=True)
        for b in range(nb):
            part = dot(kvbuf[h, 1, k0 + b * KB : k0 + (b + 1) * KB, :], dot_t)
            shares = s_buf[b * KB : (b + 1) * KB, :] * inverse
            ds_buf[b * KB : (b + 1) * KB, :] = (shares * (part - delta) * score_scale).astype(BF16)
        dqt = dot(knt[:, k0 : k0 + SPAN], ds_buf[...])
        dk = dot(ds_buf[...], jnp.transpose(qt))
        dv = dot(p_buf[...], do)
        if g == 0 and j == 0:
            dkacc[0:SPAN, :] = dk
            dvacc[0:SPAN, :] = dv
        elif g == 0:
            old = SPAN - QB
            dkacc[k0 : k0 + old, :] += dk[:old]
            dvacc[k0 : k0 + old, :] += dv[:old]
            dkacc[k0 + old : k0 + SPAN, :] = dk[old:]
            dvacc[k0 + old : k0 + SPAN, :] = dv[old:]
        else:
            dkacc[k0 : k0 + SPAN, :] += dk
            dvacc[k0 : k0 + SPAN, :] += dv
        gs = dqt * gain
        lean = jnp.mean(gs * xt, axis=0, keepdims=True)
        dx = gs * r - xt * (r * r * r * lean)
        dqbuf[h, rows, cols] = jnp.transpose(dx.astype(BF16))
        qsacc[...] += dqt * xr

    def send_parts(h):
        far_k = dkacc[0:T, :].astype(BF16)
        g2send[h, 0] = far_k
        g2send[h, 1] = dvacc[0:T, :].astype(BF16)
        grad_far(h).start()
        near_k = dkacc[T : 2 * T, :].astype(BF16)
        g1buf[h, 0] = near_k
        g1buf[h, 1] = dvacc[T : 2 * T, :].astype(BF16)
        own_k = dkacc[2 * T : 3 * T, :]
        own[h, 0] = own_k
        own[h, 1] = dvacc[2 * T : 3 * T, :]
        ksacc[...] += (
            fold_rows(far_k.astype(F32) * khat[0:T, :], jnp.sum)
            + fold_rows(near_k.astype(F32) * khat[T : 2 * T, :], jnp.sum)
            + fold_rows(own_k * khat[2 * T : 3 * T, :], jnp.sum)
        )

    def merge(h):
        grad_far(h).wait_recv()
        g1buf[h] = (g1buf[h].astype(F32) + g2recv[h].astype(F32)).astype(BF16)
        grad_near(h).start()

    def finish(h):
        grad_near(h).wait_recv()
        dkvout[h, 1] = (own[h, 1] + g1recv[h, 1].astype(F32)).astype(BF16)
        grad = own[h, 0] + g1recv[h, 0].astype(F32)
        x = kvbuf[h, 0, pl.ds(2 * T, T), :].astype(F32)
        r = lax.rsqrt(jnp.mean(x * x, axis=1, keepdims=True) + norm_eps)
        gs = grad * krow
        lean = jnp.mean(gs * x, axis=1, keepdims=True)
        dkvout[h, 0] = (gs * r - x * (r * r * r * lean)).astype(BF16)
        for copy in key_stores(h):
            copy.start()

    def step(h, carry):
        @pl.when(h + 1 < heads)
        def _():
            relay(h + 1)

        @pl.when(h + 3 < heads)
        def _():
            start_halo(h + 3)

        for copy in load_copies(h):
            copy.wait()
        halo_far(h).wait_recv()
        prepare(h)
        for g in range(2):
            for j in range(T // QB):
                unit(h, g, j)
        send_parts(h)
        for copy in query_stores(h):
            copy.start()

        @pl.when(h >= 1)
        def _():
            merge(h - 1)

        @pl.when(h >= 2)
        def _():
            finish(h - 2)

        return carry

    lax.fori_loop(0, heads, step, 0)

    query_part = jnp.sum(jnp.transpose(qsacc[...]), axis=0, keepdims=True)
    key_part = jnp.sum(ksacc[...], axis=0, keepdims=True)
    row = lax.broadcasted_iota(jnp.int32, (8, HD), 0)
    stage_start(0, jnp.where(row == 0, query_part, jnp.where(row == 1, key_part, 0.0)))
    merge(heads - 1)
    finish(heads - 2)
    stage_start(1, stage_sum(0))
    stage_start(2, stage_sum(1))
    finish(heads - 1)
    totals = stage_sum(2)
    qsg_ref[...] = totals[0:1]
    ksg_ref[...] = totals[1:2]

    def drain(h, carry):
        for copy in halo_near(h):
            copy.wait_send()
        halo_far(h).wait_send()
        grad_far(h).wait_send()
        grad_near(h).wait_send()
        for copy in query_stores(h) + key_stores(h):
            copy.wait()
        return carry

    lax.fori_loop(0, heads, drain, 0)


def body(mesh_shape, query_raw, key_raw, values, out_grad, query_scale, key_scale, block_doc, doc_end):
    ctx_size, dp_size, inner = mesh_shape
    tokens = query_raw.shape[1]
    heads = key_raw.shape[2] // HD
    outer = ctx_size // inner
    exchanges = dp_size + inner + outer - 3
    any_spec = pl.BlockSpec(memory_space=pl.ANY)
    vmem_spec = pl.BlockSpec(memory_space=pltpu.VMEM)
    smem_spec = pl.BlockSpec(memory_space=pltpu.SMEM)
    dma = pltpu.SemaphoreType.DMA
    wide = jax.ShapeDtypeStruct((tokens, 2 * heads * HD), BF16)
    narrow = jax.ShapeDtypeStruct((tokens, heads * HD), BF16)
    gain = jax.ShapeDtypeStruct((1, HD), F32)
    attended, query_grad, key_grad, value_grad, query_gain, key_gain = pl.pallas_call(
        functools.partial(kernel, heads, ctx_size, dp_size, inner),
        out_shape=(wide, wide, narrow, narrow, gain, gain),
        in_specs=[any_spec] * 4 + [vmem_spec] * 2 + [smem_spec] * 2,
        out_specs=[any_spec] * 4 + [vmem_spec] * 2,
        scratch_shapes=[
            pltpu.VMEM((heads, T, 2 * HD), BF16),
            pltpu.VMEM((heads, T, 2 * HD), BF16),
            pltpu.VMEM((heads, 2, 3 * T, HD), BF16),
            pltpu.VMEM((heads, T, 2 * HD), BF16),
            pltpu.VMEM((heads, T, 2 * HD), BF16),
            pltpu.VMEM((heads, 2, T, HD), BF16),
            pltpu.VMEM((3 * T, HD), BF16),
            pltpu.VMEM((HD, 3 * T), BF16),
            pltpu.VMEM((HD, 3 * T), BF16),
            pltpu.VMEM((3 * T, HD), F32),
            pltpu.VMEM((HD, QB), F32),
            pltpu.VMEM((SPAN, QB), F32),
            pltpu.VMEM((SPAN, QB), BF16),
            pltpu.VMEM((SPAN, QB), BF16),
            pltpu.VMEM((3 * T, HD), F32),
            pltpu.VMEM((3 * T, HD), F32),
            pltpu.VMEM((heads, 2, T, HD), F32),
            pltpu.VMEM((heads, 2, T, HD), BF16),
            pltpu.VMEM((heads, 2, T, HD), BF16),
            pltpu.VMEM((heads, 2, T, HD), BF16),
            pltpu.VMEM((heads, 2, T, HD), BF16),
            pltpu.VMEM((HD, QB), F32),
            pltpu.VMEM((8, HD), F32),
            pltpu.VMEM((dp_size, 8, HD), F32),
            pltpu.VMEM((inner, 8, HD), F32),
            pltpu.VMEM((outer, 8, HD), F32),
            dma((heads, 4)),
            dma((heads, 4)),
            dma((heads, 2)),
            dma((heads, 2)),
            dma((heads,)),
            dma((heads,)),
            dma((heads,)),
            dma((heads,)),
            dma((heads,)),
            dma((heads,)),
            dma((exchanges,)),
            dma((exchanges,)),
        ],
        compiler_params=pltpu.CompilerParams(
            collective_id=0, has_side_effects=True, vmem_limit_bytes=VMEM_LIMIT
        ),
    )(
        query_raw[0],
        key_raw[0],
        values[0],
        out_grad[0],
        query_scale.reshape(1, HD),
        key_scale.reshape(1, HD),
        block_doc,
        doc_end,
    )
    return (
        attended[None],
        query_grad[None],
        key_grad[None],
        value_grad[None],
        query_gain.reshape(HD),
        key_gain.reshape(HD),
    )


def solution(mesh):
    ctx_size = mesh.shape["ctx"]
    dp_size = mesh.shape["dp"]
    inner = 4 if ctx_size % 4 == 0 else 1
    row = P("dp", "ctx", None)
    return jax.shard_map(
        functools.partial(body, (ctx_size, dp_size, inner)),
        mesh=mesh,
        in_specs=(row, row, row, row, P(), P(), P("dp", None), P("dp", None)),
        out_specs=(row, row, row, row, P(), P()),
        check_vma=False,
    )
```

```python
import functools

import jax
import jax.numpy as jnp
from jax import lax
from jax.experimental import pallas as pl
from jax.experimental.pallas import tpu as pltpu
from jax.sharding import PartitionSpec as P

WINDOW = 1024
BLOCK = 1024
MESH = pl.DeviceIdType.MESH
F32 = jnp.float32
BF16 = jnp.bfloat16

score_scale = 168.0 ** (-0.5)
LOG2E = 1.4426950408889634
norm_eps = 1e-06
MASKED = -1e30

HD = 128
T = 512
QB = 256
KB = 256
SPAN = WINDOW + QB
VMEM_LIMIT = 44 * 1024 * 1024
NEAR_AHEAD = 3
FINISH_LAG = 3


def dot(a, b):
    return lax.dot_general(a, b, (((1,), (0,)), ((), ())), preferred_element_type=F32)


def fold_rows(x, op):
    return op(x.reshape(x.shape[0] // 8, 8, x.shape[1]), axis=0)


def kernel(
    heads,
    ctx_size,
    dp_size,
    inner,
    q_hbm,
    k_hbm,
    v_hbm,
    do_hbm,
    qs_hbm,
    ks_hbm,
    doc_hbm,
    end_hbm,
    att_hbm,
    dq_hbm,
    dk_hbm,
    dv_hbm,
    gains_hbm,
    qbuf,
    dobuf,
    kvbuf,
    attbuf,
    dqbuf,
    dkvout,
    kn,
    knt,
    vt,
    khat,
    qst,
    s_buf,
    p_buf,
    ds_buf,
    dkacc,
    dvacc,
    own,
    g2send,
    g1buf,
    g2recv,
    g1recv,
    qsacc,
    ksacc,
    ar1,
    ar2,
    gains,
    scales,
    docs,
    small_sem,
    load_sem,
    store_sem,
    a_send,
    a_recv,
    r_send,
    r_recv,
    g2_send,
    g2_recv,
    g1_send,
    g1_recv,
    ar_send,
    ar_recv,
):
    me = lax.axis_index("ctx")
    dp = lax.axis_index("dp")
    nxt = lax.rem(me + 1, ctx_size)
    prv = lax.rem(me + ctx_size - 1, ctx_size)
    last = heads - 1
    outer = ctx_size // inner
    me_in = lax.rem(me, inner)
    me_out = me // inner

    def load_copies(h):
        wide = pl.ds(pl.multiple_of(h * 2 * HD, 2 * HD), 2 * HD)
        narrow = pl.ds(pl.multiple_of(h * HD, HD), HD)
        return (
            pltpu.make_async_copy(k_hbm.at[:, narrow], kvbuf.at[h, 0, pl.ds(2 * T, T)], load_sem.at[h, 0]),
            pltpu.make_async_copy(v_hbm.at[:, narrow], kvbuf.at[h, 1, pl.ds(2 * T, T)], load_sem.at[h, 1]),
            pltpu.make_async_copy(q_hbm.at[:, wide], qbuf.at[h], load_sem.at[h, 2]),
            pltpu.make_async_copy(do_hbm.at[:, wide], dobuf.at[h], load_sem.at[h, 3]),
        )

    def query_stores(h):
        wide = pl.ds(pl.multiple_of(h * 2 * HD, 2 * HD), 2 * HD)
        return (
            pltpu.make_async_copy(attbuf.at[h], att_hbm.at[:, wide], store_sem.at[h, 0]),
            pltpu.make_async_copy(dqbuf.at[h], dq_hbm.at[:, wide], store_sem.at[h, 1]),
        )

    def key_stores(h):
        narrow = pl.ds(pl.multiple_of(h * HD, HD), HD)
        return (
            pltpu.make_async_copy(dkvout.at[h, 0], dk_hbm.at[:, narrow], store_sem.at[h, 2]),
            pltpu.make_async_copy(dkvout.at[h, 1], dv_hbm.at[:, narrow], store_sem.at[h, 3]),
        )

    def remote(src, dst, send, recv, device):
        return pltpu.make_async_remote_copy(
            src_ref=src, dst_ref=dst, send_sem=send, recv_sem=recv, device_id=device, device_id_type=MESH
        )

    def halo_near(h, half):
        narrow = pl.ds(pl.multiple_of(h * HD, HD), HD)
        source = pl.ds(half * QB, QB)
        place = pl.ds(T + half * QB, QB)
        return [
            remote(
                hbm.at[source, narrow],
                kvbuf.at[h, kv, place],
                a_send.at[h, half, kv],
                a_recv.at[h, half, kv],
                {"ctx": nxt},
            )
            for kv, hbm in enumerate((k_hbm, v_hbm))
        ]

    def halo_far(h, half):
        return remote(
            kvbuf.at[h, :, pl.ds(T + half * QB, QB)],
            kvbuf.at[h, :, pl.ds(half * QB, QB)],
            r_send.at[h, half],
            r_recv.at[h, half],
            {"ctx": nxt},
        )

    def grad_far(h, kv):
        return remote(g2send.at[h, kv], g2recv.at[h, kv], g2_send.at[h, kv], g2_recv.at[h, kv], {"ctx": prv})

    def grad_near(h, kv):
        return remote(g1buf.at[h, kv], g1recv.at[h, kv], g1_send.at[h, kv], g1_recv.at[h, kv], {"ctx": prv})

    def partners(stage):
        if stage == 0:
            return [
                {"dp": lax.rem(dp + d, dp_size), "ctx": me_out * inner + lax.rem(me_in + c, inner)}
                for d in range(dp_size)
                for c in range(inner)
                if d or c
            ]
        return [{"ctx": lax.rem(me_out + d, outer) * inner + me_in} for d in range(1, outer)]

    stage_slot = (dp * inner + me_in, me_out)
    stage_buf = (ar1, ar2)
    stage_base = (0, dp_size * inner - 1)

    def stage_copies(stage):
        slot = stage_buf[stage].at[stage_slot[stage]]
        base = stage_base[stage]
        return [
            remote(slot, slot, ar_send.at[base + d], ar_recv.at[base + d], device)
            for d, device in enumerate(partners(stage))
        ]

    def stage_start(stage, value):
        stage_buf[stage][stage_slot[stage]] = value
        for copy in stage_copies(stage):
            copy.start()

    def stage_sum(stage):
        for copy in stage_copies(stage):
            copy.wait()
        total = stage_buf[stage][0]
        for slot in range(1, stage_buf[stage].shape[0]):
            total = total + stage_buf[stage][slot]
        return total

    small_copies = (
        pltpu.make_async_copy(qs_hbm, scales.at[pl.ds(0, 1)], small_sem.at[0]),
        pltpu.make_async_copy(ks_hbm, scales.at[pl.ds(1, 1)], small_sem.at[1]),
        pltpu.make_async_copy(doc_hbm, docs.at[pl.ds(0, 1)], small_sem.at[2]),
        pltpu.make_async_copy(end_hbm, docs.at[pl.ds(1, 1)], small_sem.at[3]),
    )
    for copy in small_copies:
        copy.start()

    def start_loads(h, carry):
        for copy in load_copies(h):
            copy.start()
        return carry

    lax.fori_loop(0, heads, start_loads, 0)

    barrier = pltpu.get_barrier_semaphore()
    greeted = [{"ctx": nxt}, {"ctx": prv}] + partners(0) + partners(1)
    for device in greeted:
        pl.semaphore_signal(barrier, inc=1, device_id=device, device_id_type=MESH)
    pl.semaphore_wait(barrier, len(greeted))

    def start_halo(h):
        for half in (1, 0):
            for copy in halo_near(h, half):
                copy.start()

    def relay(h):
        for half in (1, 0):
            for copy in halo_near(h, half):
                copy.wait_recv()
            halo_far(h, half).start()

    start_halo(0)
    relay(0)
    for h in range(1, min(NEAR_AHEAD, heads)):
        start_halo(h)

    for copy in small_copies:
        copy.wait()
    qrow = scales[0:1, :]
    krow = scales[1:2, :]
    half = jnp.transpose(jnp.broadcast_to(qrow, (HD, HD)))
    qst[...] = jnp.concatenate([half, half], axis=1)
    qsacc[...] = jnp.zeros_like(qsacc)
    ksacc[...] = jnp.zeros_like(ksacc)

    block = me * T // BLOCK
    doc = docs[0, block]
    before = docs[0, jnp.maximum(block - 1, 0)]
    same = (block > 0) & (doc == before)
    into = me * T - block * BLOCK
    first = jnp.where(same, 0, 2 * T - into)
    limit = docs[1, doc] - (me - 2) * T

    def prepare(h, b):
        rows = slice(b * KB, (b + 1) * KB)
        x = kvbuf[h, 0, rows, :].astype(F32)
        mean_square = jnp.mean(x * x, axis=1, keepdims=True)
        hat = x * lax.rsqrt(mean_square + norm_eps)
        khat[rows, :] = hat
        normed = (hat * krow).astype(BF16)
        kn[rows, :] = normed
        knt[:, rows] = jnp.transpose(normed)
        vt[:, rows] = jnp.transpose(kvbuf[h, 1, rows, :])

    def unit(h, g, j):
        rows = pl.ds(j * QB, QB)
        cols = pl.ds(g * HD, HD)
        k0 = j * QB
        nb = SPAN // KB
        gain = qst[...]
        xt = jnp.transpose(qbuf[h, rows, cols].astype(F32))
        mean_square = jnp.mean(xt * xt, axis=0, keepdims=True)
        r = lax.rsqrt(mean_square + norm_eps)
        xr = xt * r
        qt = (xr * gain).astype(BF16)
        do = dobuf[h, rows, cols]
        dot_t = jnp.transpose(do)
        lane = lax.broadcasted_iota(jnp.int32, (1, QB), 1)
        low = jnp.maximum(first, k0 + 1 + lane)
        high = jnp.minimum(limit, k0 + 1 + WINDOW + lane)
        place = lax.broadcasted_iota(jnp.int32, (KB, QB), 0)
        peak = jnp.full((8, QB), MASKED, F32)
        for b in range(nb):
            keys = kn[k0 + b * KB : k0 + (b + 1) * KB, :]
            s = dot(keys, qt)
            spot = place + (k0 + b * KB)
            s = jnp.where((spot >= low) & (spot < high), s, MASKED)
            s_buf[b * KB : (b + 1) * KB, :] = s
            peak = jnp.maximum(peak, fold_rows(s, jnp.max))
        peak = jnp.max(peak, axis=0, keepdims=True)
        total = jnp.zeros((8, QB), F32)
        for b in range(nb):
            e = jnp.exp2((s_buf[b * KB : (b + 1) * KB, :] - peak) * (score_scale * LOG2E))
            s_buf[b * KB : (b + 1) * KB, :] = e
            total = total + fold_rows(e, jnp.sum)
        inverse = 1.0 / jnp.sum(total, axis=0, keepdims=True)
        for b in range(nb):
            p_buf[b * KB : (b + 1) * KB, :] = (s_buf[b * KB : (b + 1) * KB, :] * inverse).astype(BF16)
        o = dot(vt[:, k0 : k0 + SPAN], p_buf[...]).astype(BF16)
        attbuf[h, rows, cols] = jnp.transpose(o)
        delta = jnp.sum(dot_t.astype(F32) * o.astype(F32), axis=0, keepdims=True)
        for b in range(nb):
            part = dot(kvbuf[h, 1, k0 + b * KB : k0 + (b + 1) * KB, :], dot_t)
            shares = s_buf[b * KB : (b + 1) * KB, :] * inverse
            ds_buf[b * KB : (b + 1) * KB, :] = (shares * (part - delta) * score_scale).astype(BF16)
        dqt = dot(knt[:, k0 : k0 + SPAN], ds_buf[...])
        dk = dot(ds_buf[...], jnp.transpose(qt))
        dv = dot(p_buf[...], do)
        if g == 0 and j == 1:
            dkacc[k0 : k0 + SPAN, :] = dk
            dvacc[k0 : k0 + SPAN, :] = dv
        elif g == 0:
            dkacc[0:QB, :] = dk[:QB]
            dvacc[0:QB, :] = dv[:QB]
            dkacc[QB:SPAN, :] += dk[QB:]
            dvacc[QB:SPAN, :] += dv[QB:]
        else:
            dkacc[k0 : k0 + SPAN, :] += dk
            dvacc[k0 : k0 + SPAN, :] += dv
        gs = dqt * gain
        lean = jnp.mean(gs * xt, axis=0, keepdims=True)
        dx = gs * r - xt * (r * r * r * lean)
        dqbuf[h, rows, cols] = jnp.transpose(dx.astype(BF16))
        qsacc[...] += dqt * xr

    def send_parts(h):
        g2send[h, 1] = dvacc[0:T, :].astype(BF16)
        grad_far(h, 1).start()
        far_k = dkacc[0:T, :].astype(BF16)
        g2send[h, 0] = far_k
        grad_far(h, 0).start()
        near_k = dkacc[T : 2 * T, :].astype(BF16)
        g1buf[h, 0] = near_k
        g1buf[h, 1] = dvacc[T : 2 * T, :].astype(BF16)
        own_k = dkacc[2 * T : 3 * T, :]
        own[h, 0] = own_k
        own[h, 1] = dvacc[2 * T : 3 * T, :]
        ksacc[...] += (
            fold_rows(far_k.astype(F32) * khat[0:T, :], jnp.sum)
            + fold_rows(near_k.astype(F32) * khat[T : 2 * T, :], jnp.sum)
            + fold_rows(own_k * khat[2 * T : 3 * T, :], jnp.sum)
        )

    def merge(h):
        for kv in (1, 0):
            grad_far(h, kv).wait_recv()
            g1buf[h, kv] = (g1buf[h, kv].astype(F32) + g2recv[h, kv].astype(F32)).astype(BF16)
            grad_near(h, kv).start()

    def finish(h):
        grad_near(h, 1).wait_recv()
        dkvout[h, 1] = (own[h, 1] + g1recv[h, 1].astype(F32)).astype(BF16)
        grad_near(h, 0).wait_recv()
        total_k = own[h, 0] + g1recv[h, 0].astype(F32)
        x = kvbuf[h, 0, pl.ds(2 * T, T), :].astype(F32)
        r = lax.rsqrt(jnp.mean(x * x, axis=1, keepdims=True) + norm_eps)
        gs = total_k * krow
        lean = jnp.mean(gs * x, axis=1, keepdims=True)
        dkvout[h, 0] = (gs * r - x * (r * r * r * lean)).astype(BF16)
        for copy in key_stores(h):
            copy.start()

    def hand_on(h):
        @pl.when(h + 1 < heads)
        def _():
            relay(h + 1)

        @pl.when(h + NEAR_AHEAD < heads)
        def _():
            start_halo(h + NEAR_AHEAD)

    def step(h, carry):
        for copy in load_copies(h):
            copy.wait()
        halo_far(h, 1).wait_recv()

        @pl.when(h > 0)
        def _():
            hand_on(h)

        for b in range(1, 3 * T // KB):
            prepare(h, b)
        unit(h, 0, 1)
        unit(h, 1, 1)

        @pl.when(h == last)
        def _():
            merge(h - 1)

        halo_far(h, 0).wait_recv()
        prepare(h, 0)
        unit(h, 0, 0)
        unit(h, 1, 0)
        send_parts(h)
        for copy in query_stores(h):
            copy.start()

        @pl.when(h == 0)
        def _():
            hand_on(h)

        @pl.when((h >= 1) & (h < last))
        def _():
            merge(h - 1)

        @pl.when(h >= FINISH_LAG)
        def _():
            finish(h - FINISH_LAG)

        return carry

    lax.fori_loop(0, heads, step, 0)

    query_part = jnp.sum(jnp.transpose(qsacc[...]), axis=0, keepdims=True)
    key_part = jnp.sum(ksacc[...], axis=0, keepdims=True)
    row = lax.broadcasted_iota(jnp.int32, (8, HD), 0)
    stage_start(0, jnp.where(row == 0, query_part, jnp.where(row == 1, key_part, 0.0)))
    for h in range(heads - FINISH_LAG, heads - 2):
        finish(h)
    merge(last)
    finish(last - 1)
    stage_start(1, stage_sum(0))
    gains[...] = stage_sum(1)
    gains_copy = pltpu.make_async_copy(gains, gains_hbm, small_sem.at[0])
    gains_copy.start()
    finish(last)

    def drain(h, carry):
        for half in range(2):
            for copy in halo_near(h, half):
                copy.wait_send()
            halo_far(h, half).wait_send()
            grad_far(h, half).wait_send()
            grad_near(h, half).wait_send()
        for copy in query_stores(h) + key_stores(h):
            copy.wait()
        return carry

    lax.fori_loop(0, heads, drain, 0)
    gains_copy.wait()


def flush(*refs):
    sources, targets, sem = refs[:5], refs[5:11], refs[11]
    copies = [
        pltpu.make_async_copy(source, target, sem.at[i])
        for i, (source, target) in enumerate(zip(sources[:4], targets[:4]))
    ]
    copies.append(pltpu.make_async_copy(sources[4].at[pl.ds(0, 1)], targets[4], sem.at[4]))
    copies.append(pltpu.make_async_copy(sources[4].at[pl.ds(1, 1)], targets[5], sem.at[5]))
    for copy in copies:
        copy.start()
    for copy in copies:
        copy.wait()


def body(mesh_shape, query_raw, key_raw, values, out_grad, query_scale, key_scale, block_doc, doc_end):
    ctx_size, dp_size, inner = mesh_shape
    tokens = query_raw.shape[1]
    blocks = block_doc.shape[1]
    heads = key_raw.shape[2] // HD
    outer = ctx_size // inner
    exchanges = dp_size * inner + outer - 2
    any_spec = pl.BlockSpec(memory_space=pl.ANY)
    hbm_spec = pl.BlockSpec(memory_space=pltpu.HBM)
    dma = pltpu.SemaphoreType.DMA
    wide = jax.ShapeDtypeStruct((tokens, 2 * heads * HD), BF16)
    narrow = jax.ShapeDtypeStruct((tokens, heads * HD), BF16)
    gain = jax.ShapeDtypeStruct((1, HD), F32)
    inputs = [
        pltpu.with_memory_space_constraint(x, pltpu.HBM)
        for x in (
            query_raw[0],
            key_raw[0],
            values[0],
            out_grad[0],
            query_scale.reshape(1, HD),
            key_scale.reshape(1, HD),
            block_doc,
            doc_end,
        )
    ]
    results = pl.pallas_call(
        functools.partial(kernel, heads, ctx_size, dp_size, inner),
        out_shape=(wide, wide, narrow, narrow, jax.ShapeDtypeStruct((8, HD), F32)),
        in_specs=[hbm_spec] * 8,
        out_specs=[any_spec] * 5,
        scratch_shapes=[
            pltpu.VMEM((heads, T, 2 * HD), BF16),
            pltpu.VMEM((heads, T, 2 * HD), BF16),
            pltpu.VMEM((heads, 2, 3 * T, HD), BF16),
            pltpu.VMEM((heads, T, 2 * HD), BF16),
            pltpu.VMEM((heads, T, 2 * HD), BF16),
            pltpu.VMEM((heads, 2, T, HD), BF16),
            pltpu.VMEM((3 * T, HD), BF16),
            pltpu.VMEM((HD, 3 * T), BF16),
            pltpu.VMEM((HD, 3 * T), BF16),
            pltpu.VMEM((3 * T, HD), F32),
            pltpu.VMEM((HD, QB), F32),
            pltpu.VMEM((SPAN, QB), F32),
            pltpu.VMEM((SPAN, QB), BF16),
            pltpu.VMEM((SPAN, QB), BF16),
            pltpu.VMEM((3 * T, HD), F32),
            pltpu.VMEM((3 * T, HD), F32),
            pltpu.VMEM((heads, 2, T, HD), F32),
            pltpu.VMEM((heads, 2, T, HD), BF16),
            pltpu.VMEM((heads, 2, T, HD), BF16),
            pltpu.VMEM((heads, 2, T, HD), BF16),
            pltpu.VMEM((heads, 2, T, HD), BF16),
            pltpu.VMEM((HD, QB), F32),
            pltpu.VMEM((8, HD), F32),
            pltpu.VMEM((dp_size * inner, 8, HD), F32),
            pltpu.VMEM((outer, 8, HD), F32),
            pltpu.VMEM((8, HD), F32),
            pltpu.VMEM((2, HD), F32),
            pltpu.SMEM((2, blocks), jnp.int32),
            dma((4,)),
            dma((heads, 4)),
            dma((heads, 4)),
            dma((heads, 2, 2)),
            dma((heads, 2, 2)),
            dma((heads, 2)),
            dma((heads, 2)),
            dma((heads, 2)),
            dma((heads, 2)),
            dma((heads, 2)),
            dma((heads, 2)),
            dma((exchanges,)),
            dma((exchanges,)),
        ],
        compiler_params=pltpu.CompilerParams(
            collective_id=0, has_side_effects=True, vmem_limit_bytes=VMEM_LIMIT
        ),
    )(*inputs)
    attended, query_grad, key_grad, value_grad, query_gain, key_gain = pl.pallas_call(
        flush,
        out_shape=(wide, wide, narrow, narrow, gain, gain),
        in_specs=[any_spec] * 5,
        out_specs=[any_spec] * 6,
        scratch_shapes=[dma((6,))],
        compiler_params=pltpu.CompilerParams(vmem_limit_bytes=1024 * 1024),
    )(*results)
    return (
        attended[None],
        query_grad[None],
        key_grad[None],
        value_grad[None],
        query_gain.reshape(HD),
        key_gain.reshape(HD),
    )


def solution(mesh):
    ctx_size = mesh.shape["ctx"]
    dp_size = mesh.shape["dp"]
    inner = 4 if ctx_size % 4 == 0 else 1
    row = P("dp", "ctx", None)
    return jax.shard_map(
        functools.partial(body, (ctx_size, dp_size, inner)),
        mesh=mesh,
        in_specs=(row, row, row, row, P(), P(), P("dp", None), P("dp", None)),
        out_specs=(row, row, row, row, P(), P()),
        check_vma=False,
    )
```

```python
import functools

import jax
import jax.numpy as jnp
from jax import lax
from jax.experimental import pallas as pl
from jax.experimental.pallas import tpu as pltpu
from jax.sharding import PartitionSpec as P

WINDOW = 1024
BLOCK = 1024
MESH = pl.DeviceIdType.MESH
F32 = jnp.float32
BF16 = jnp.bfloat16

score_scale = 168.0 ** (-0.5)
LOG2E = 1.4426950408889634
norm_eps = 1e-06
MASKED = -1e30

HD = 128
T = 512
QB = 256
KB = 256
SPAN = WINDOW + QB
VMEM_LIMIT = 46 * 1024 * 1024
NEAR_AHEAD = 3
FINISH_LAG = 3


def dot(a, b):
    return lax.dot_general(a, b, (((1,), (0,)), ((), ())), preferred_element_type=F32)


def fold_rows(x, op):
    return op(x.reshape(x.shape[0] // 8, 8, x.shape[1]), axis=0)


def kernel(
    heads,
    ctx_size,
    dp_size,
    inner,
    q_hbm,
    k_hbm,
    v_hbm,
    do_hbm,
    qs_hbm,
    ks_hbm,
    doc_hbm,
    end_hbm,
    att_hbm,
    dq_hbm,
    dk_hbm,
    dv_hbm,
    gains_hbm,
    qbuf,
    dobuf,
    kvbuf,
    attbuf,
    dqbuf,
    dkvout,
    kn,
    knt,
    vt,
    khat,
    qst,
    s_buf,
    p_buf,
    ds_buf,
    dkacc,
    dvacc,
    own,
    g2send,
    g1buf,
    g2recv,
    g1recv,
    qsacc,
    ksacc,
    ar1,
    ar2,
    gains,
    scales,
    docs,
    small_sem,
    load_sem,
    store_sem,
    a_send,
    a_recv,
    r_send,
    r_recv,
    g2_send,
    g2_recv,
    g1_send,
    g1_recv,
    ar_send,
    ar_recv,
):
    me = lax.axis_index("ctx")
    dp = lax.axis_index("dp")
    nxt = lax.rem(me + 1, ctx_size)
    prv = lax.rem(me + ctx_size - 1, ctx_size)
    last = heads - 1
    outer = ctx_size // inner
    me_in = lax.rem(me, inner)
    me_out = me // inner

    def load_copies(h):
        wide = pl.ds(pl.multiple_of(h * 2 * HD, 2 * HD), 2 * HD)
        narrow = pl.ds(pl.multiple_of(h * HD, HD), HD)
        return (
            pltpu.make_async_copy(k_hbm.at[:, narrow], kvbuf.at[h, 0, pl.ds(2 * T, T)], load_sem.at[h, 0]),
            pltpu.make_async_copy(v_hbm.at[:, narrow], kvbuf.at[h, 1, pl.ds(2 * T, T)], load_sem.at[h, 1]),
            pltpu.make_async_copy(q_hbm.at[:, wide], qbuf.at[h], load_sem.at[h, 2]),
            pltpu.make_async_copy(do_hbm.at[:, wide], dobuf.at[h], load_sem.at[h, 3]),
        )

    def query_stores(h):
        wide = pl.ds(pl.multiple_of(h * 2 * HD, 2 * HD), 2 * HD)
        return (
            pltpu.make_async_copy(attbuf.at[h], att_hbm.at[:, wide], store_sem.at[h, 0]),
            pltpu.make_async_copy(dqbuf.at[h], dq_hbm.at[:, wide], store_sem.at[h, 1]),
        )

    def key_stores(h):
        narrow = pl.ds(pl.multiple_of(h * HD, HD), HD)
        return (
            pltpu.make_async_copy(dkvout.at[h, 0], dk_hbm.at[:, narrow], store_sem.at[h, 2]),
            pltpu.make_async_copy(dkvout.at[h, 1], dv_hbm.at[:, narrow], store_sem.at[h, 3]),
        )

    def remote(src, dst, send, recv, device):
        return pltpu.make_async_remote_copy(
            src_ref=src, dst_ref=dst, send_sem=send, recv_sem=recv, device_id=device, device_id_type=MESH
        )

    def halo_near(h, half):
        narrow = pl.ds(pl.multiple_of(h * HD, HD), HD)
        source = pl.ds(half * QB, QB)
        place = pl.ds(T + half * QB, QB)
        return [
            remote(
                hbm.at[source, narrow],
                kvbuf.at[h, kv, place],
                a_send.at[h, half, kv],
                a_recv.at[h, half, kv],
                {"ctx": nxt},
            )
            for kv, hbm in enumerate((k_hbm, v_hbm))
        ]

    def halo_far(h, half):
        return remote(
            kvbuf.at[h, :, pl.ds(T + half * QB, QB)],
            kvbuf.at[h, :, pl.ds(half * QB, QB)],
            r_send.at[h, half],
            r_recv.at[h, half],
            {"ctx": nxt},
        )

    def grad_far(h, kv):
        return remote(g2send.at[h, kv], g2recv.at[h, kv], g2_send.at[h, kv], g2_recv.at[h, kv], {"ctx": prv})

    def grad_near(h, kv):
        return remote(g1buf.at[h, kv], g1recv.at[h, kv], g1_send.at[h, kv], g1_recv.at[h, kv], {"ctx": prv})

    def partners(stage):
        if stage == 0:
            return [
                {"dp": lax.rem(dp + d, dp_size), "ctx": me_out * inner + lax.rem(me_in + c, inner)}
                for d in range(dp_size)
                for c in range(inner)
                if d or c
            ]
        return [{"ctx": lax.rem(me_out + d, outer) * inner + me_in} for d in range(1, outer)]

    stage_slot = (dp * inner + me_in, me_out)
    stage_buf = (ar1, ar2)
    stage_base = (0, dp_size * inner - 1)

    def stage_copies(stage):
        slot = stage_buf[stage].at[stage_slot[stage]]
        base = stage_base[stage]
        return [
            remote(slot, slot, ar_send.at[base + d], ar_recv.at[base + d], device)
            for d, device in enumerate(partners(stage))
        ]

    def stage_start(stage, value):
        stage_buf[stage][stage_slot[stage]] = value
        for copy in stage_copies(stage):
            copy.start()

    def stage_sum(stage):
        for copy in stage_copies(stage):
            copy.wait()
        total = stage_buf[stage][0]
        for slot in range(1, stage_buf[stage].shape[0]):
            total = total + stage_buf[stage][slot]
        return total

    small_copies = (
        pltpu.make_async_copy(qs_hbm, scales.at[pl.ds(0, 1)], small_sem.at[0]),
        pltpu.make_async_copy(ks_hbm, scales.at[pl.ds(1, 1)], small_sem.at[1]),
        pltpu.make_async_copy(doc_hbm, docs.at[pl.ds(0, 1)], small_sem.at[2]),
        pltpu.make_async_copy(end_hbm, docs.at[pl.ds(1, 1)], small_sem.at[3]),
    )
    for copy in small_copies:
        copy.start()

    def start_loads(h, carry):
        for copy in load_copies(h):
            copy.start()
        return carry

    lax.fori_loop(0, heads, start_loads, 0)

    barrier = pltpu.get_barrier_semaphore()
    greeted = [{"ctx": nxt}, {"ctx": prv}] + partners(0) + partners(1)
    for device in greeted:
        pl.semaphore_signal(barrier, inc=1, device_id=device, device_id_type=MESH)
    pl.semaphore_wait(barrier, len(greeted))

    def start_halo(h):
        for half in (1, 0):
            for copy in halo_near(h, half):
                copy.start()

    def relay(h):
        for half in (1, 0):
            for copy in halo_near(h, half):
                copy.wait_recv()
            halo_far(h, half).start()

    start_halo(0)
    relay(0)
    for h in range(1, min(NEAR_AHEAD, heads)):
        start_halo(h)

    for copy in small_copies:
        copy.wait()
    qrow = scales[0:1, :]
    krow = scales[1:2, :]
    half = jnp.transpose(jnp.broadcast_to(qrow, (HD, HD)))
    qst[...] = jnp.concatenate([half, half], axis=1)
    qsacc[...] = jnp.zeros_like(qsacc)
    ksacc[...] = jnp.zeros_like(ksacc)

    block = me * T // BLOCK
    doc = docs[0, block]
    before = docs[0, jnp.maximum(block - 1, 0)]
    same = (block > 0) & (doc == before)
    into = me * T - block * BLOCK
    first = jnp.where(same, 0, 2 * T - into)
    limit = docs[1, doc] - (me - 2) * T

    def prepare(h, b):
        rows = slice(b * KB, (b + 1) * KB)
        x = kvbuf[h, 0, rows, :].astype(F32)
        mean_square = jnp.mean(x * x, axis=1, keepdims=True)
        hat = x * lax.rsqrt(mean_square + norm_eps)
        khat[rows, :] = hat
        normed = (hat * krow).astype(BF16)
        kn[rows, :] = normed
        knt[:, rows] = jnp.transpose(normed)
        vt[:, rows] = jnp.transpose(kvbuf[h, 1, rows, :])

    def unit(h, g, j, kept):
        rows = pl.ds(j * QB, QB)
        cols = pl.ds(g * HD, HD)
        lanes = slice(g * QB, (g + 1) * QB)
        k0 = j * QB
        nb = SPAN // KB
        blocks = [slice(b * KB, (b + 1) * KB) for b in range(nb)]
        gain = qst[...]
        xt = jnp.transpose(qbuf[h, rows, cols].astype(F32))
        mean_square = jnp.mean(xt * xt, axis=0, keepdims=True)
        r = lax.rsqrt(mean_square + norm_eps)
        qt = (xt * r * gain).astype(BF16)
        dot_t = jnp.transpose(dobuf[h, rows, cols])
        kept.append(jnp.transpose(qt))
        lane = lax.broadcasted_iota(jnp.int32, (1, QB), 1)
        low = jnp.maximum(first, k0 + 1 + lane)
        high = jnp.minimum(limit, k0 + 1 + WINDOW + lane)
        place = lax.broadcasted_iota(jnp.int32, (KB, QB), 0)
        peak = jnp.full((8, QB), MASKED, F32)
        for b in range(nb):
            s = dot(kn[k0 + b * KB : k0 + (b + 1) * KB, :], qt)
            spot = place + (k0 + b * KB)
            s = jnp.where((spot >= low) & (spot < high), s, MASKED)
            s_buf[blocks[b], lanes] = s
            peak = jnp.maximum(peak, fold_rows(s, jnp.max))
        peak = jnp.max(peak, axis=0, keepdims=True)
        yield
        total = jnp.zeros((8, QB), F32)
        for b in range(nb):
            e = jnp.exp2((s_buf[blocks[b], lanes] - peak) * (score_scale * LOG2E))
            s_buf[blocks[b], lanes] = e
            total = total + fold_rows(e, jnp.sum)
        inverse = 1.0 / jnp.sum(total, axis=0, keepdims=True)
        for b in range(nb):
            p_buf[blocks[b], lanes] = (s_buf[blocks[b], lanes] * inverse).astype(BF16)
        yield
        o = dot(vt[:, k0 : k0 + SPAN], p_buf[:, lanes]).astype(BF16)
        attbuf[h, rows, cols] = jnp.transpose(o)
        delta = jnp.sum(dot_t.astype(F32) * o.astype(F32), axis=0, keepdims=True)
        for b in range(nb):
            part = dot(kvbuf[h, 1, k0 + b * KB : k0 + (b + 1) * KB, :], dot_t)
            shares = s_buf[blocks[b], lanes] * inverse
            ds_buf[blocks[b], lanes] = (shares * (part - delta) * score_scale).astype(BF16)
        yield
        dqt = dot(knt[:, k0 : k0 + SPAN], ds_buf[:, lanes])
        gs = dqt * gain
        lean = jnp.mean(gs * xt, axis=0, keepdims=True)
        dx = gs * r - xt * (r * r * r * lean)
        dqbuf[h, rows, cols] = jnp.transpose(dx.astype(BF16))
        qsacc[...] += dqt * (xt * r)
        yield

    def unit_pair(h, j):
        rows = pl.ds(j * QB, QB)
        k0 = j * QB
        kept = []
        one, two = unit(h, 0, j, kept), unit(h, 1, j, kept)
        for stage in (one, two, one, one, two, two, one, two):
            next(stage)
        queries = jnp.concatenate(kept, axis=0)
        grads = jnp.concatenate([dobuf[h, rows, 0:HD], dobuf[h, rows, HD : 2 * HD]], axis=0)
        dv = dot(p_buf[...], grads)
        dk = dot(ds_buf[...], queries)
        if j == 1:
            dkacc[k0 : k0 + SPAN, :] = dk
            dvacc[k0 : k0 + SPAN, :] = dv
        else:
            dkacc[0:QB, :] = dk[:QB]
            dvacc[0:QB, :] = dv[:QB]
            dkacc[QB:SPAN, :] += dk[QB:]
            dvacc[QB:SPAN, :] += dv[QB:]

    def send_parts(h):
        far_k = dkacc[0:T, :].astype(BF16)
        near_k = dkacc[T : 2 * T, :].astype(BF16)
        own_k = dkacc[2 * T : 3 * T, :]
        ksacc[...] += (
            fold_rows(far_k.astype(F32) * khat[0:T, :], jnp.sum)
            + fold_rows(near_k.astype(F32) * khat[T : 2 * T, :], jnp.sum)
            + fold_rows(own_k * khat[2 * T : 3 * T, :], jnp.sum)
        )
        g2send[h, 1] = dvacc[0:T, :].astype(BF16)
        g2send[h, 0] = far_k

        @pl.when(h == last)
        def _():
            query_part = jnp.sum(jnp.transpose(qsacc[...]), axis=0, keepdims=True)
            key_part = jnp.sum(ksacc[...], axis=0, keepdims=True)
            row = lax.broadcasted_iota(jnp.int32, (8, HD), 0)
            stage_start(0, jnp.where(row == 0, query_part, jnp.where(row == 1, key_part, 0.0)))

        grad_far(h, 1).start()
        grad_far(h, 0).start()
        g1buf[h, 0] = near_k
        g1buf[h, 1] = dvacc[T : 2 * T, :].astype(BF16)
        own[h, 0] = own_k
        own[h, 1] = dvacc[2 * T : 3 * T, :]

    def merge(h):
        for kv in (1, 0):
            grad_far(h, kv).wait_recv()
            g1buf[h, kv] = (g1buf[h, kv].astype(F32) + g2recv[h, kv].astype(F32)).astype(BF16)
            grad_near(h, kv).start()

    def finish(h):
        grad_near(h, 1).wait_recv()
        dkvout[h, 1] = (own[h, 1] + g1recv[h, 1].astype(F32)).astype(BF16)
        grad_near(h, 0).wait_recv()
        total_k = own[h, 0] + g1recv[h, 0].astype(F32)
        x = kvbuf[h, 0, pl.ds(2 * T, T), :].astype(F32)
        r = lax.rsqrt(jnp.mean(x * x, axis=1, keepdims=True) + norm_eps)
        gs = total_k * krow
        lean = jnp.mean(gs * x, axis=1, keepdims=True)
        dkvout[h, 0] = (gs * r - x * (r * r * r * lean)).astype(BF16)
        for copy in key_stores(h):
            copy.start()

    def hand_on(h):
        @pl.when(h + 1 < heads)
        def _():
            relay(h + 1)

        @pl.when(h + NEAR_AHEAD < heads)
        def _():
            start_halo(h + NEAR_AHEAD)

    def step(h, carry):
        for copy in load_copies(h):
            copy.wait()
        halo_far(h, 1).wait_recv()

        @pl.when(h > 0)
        def _():
            hand_on(h)

        for b in range(1, 3 * T // KB):
            prepare(h, b)
        unit_pair(h, 1)

        @pl.when(h == last)
        def _():
            merge(h - 1)

        halo_far(h, 0).wait_recv()
        prepare(h, 0)
        unit_pair(h, 0)
        send_parts(h)
        for copy in query_stores(h):
            copy.start()

        @pl.when(h == 0)
        def _():
            hand_on(h)

        @pl.when((h >= 1) & (h < last))
        def _():
            merge(h - 1)

        @pl.when(h >= FINISH_LAG)
        def _():
            finish(h - FINISH_LAG)

        return carry

    lax.fori_loop(0, heads, step, 0)

    for h in range(heads - FINISH_LAG, heads - 2):
        finish(h)
    stage_start(1, stage_sum(0))
    merge(last)
    finish(last - 1)
    gains[...] = stage_sum(1)
    gains_copy = pltpu.make_async_copy(gains, gains_hbm, small_sem.at[0])
    gains_copy.start()
    finish(last)

    def drain(h, carry):
        for half in range(2):
            for copy in halo_near(h, half):
                copy.wait_send()
            halo_far(h, half).wait_send()
            grad_far(h, half).wait_send()
            grad_near(h, half).wait_send()
        for copy in query_stores(h) + key_stores(h):
            copy.wait()
        return carry

    lax.fori_loop(0, heads, drain, 0)
    gains_copy.wait()


def flush(*refs):
    sources, targets, sem = refs[:5], refs[5:11], refs[11]
    copies = [
        pltpu.make_async_copy(source, target, sem.at[i])
        for i, (source, target) in enumerate(zip(sources[:4], targets[:4]))
    ]
    copies.append(pltpu.make_async_copy(sources[4].at[pl.ds(0, 1)], targets[4], sem.at[4]))
    copies.append(pltpu.make_async_copy(sources[4].at[pl.ds(1, 1)], targets[5], sem.at[5]))
    for copy in copies:
        copy.start()
    for copy in copies:
        copy.wait()


def body(mesh_shape, query_raw, key_raw, values, out_grad, query_scale, key_scale, block_doc, doc_end):
    ctx_size, dp_size, inner = mesh_shape
    tokens = query_raw.shape[1]
    blocks = block_doc.shape[1]
    heads = key_raw.shape[2] // HD
    outer = ctx_size // inner
    exchanges = dp_size * inner + outer - 2
    any_spec = pl.BlockSpec(memory_space=pl.ANY)
    hbm_spec = pl.BlockSpec(memory_space=pltpu.HBM)
    dma = pltpu.SemaphoreType.DMA
    wide = jax.ShapeDtypeStruct((tokens, 2 * heads * HD), BF16)
    narrow = jax.ShapeDtypeStruct((tokens, heads * HD), BF16)
    gain = jax.ShapeDtypeStruct((1, HD), F32)
    inputs = [
        pltpu.with_memory_space_constraint(x, pltpu.HBM)
        for x in (
            query_raw[0],
            key_raw[0],
            values[0],
            out_grad[0],
            query_scale.reshape(1, HD),
            key_scale.reshape(1, HD),
            block_doc,
            doc_end,
        )
    ]
    results = pl.pallas_call(
        functools.partial(kernel, heads, ctx_size, dp_size, inner),
        out_shape=(wide, wide, narrow, narrow, jax.ShapeDtypeStruct((8, HD), F32)),
        in_specs=[hbm_spec] * 8,
        out_specs=[any_spec] * 5,
        scratch_shapes=[
            pltpu.VMEM((heads, T, 2 * HD), BF16),
            pltpu.VMEM((heads, T, 2 * HD), BF16),
            pltpu.VMEM((heads, 2, 3 * T, HD), BF16),
            pltpu.VMEM((heads, T, 2 * HD), BF16),
            pltpu.VMEM((heads, T, 2 * HD), BF16),
            pltpu.VMEM((heads, 2, T, HD), BF16),
            pltpu.VMEM((3 * T, HD), BF16),
            pltpu.VMEM((HD, 3 * T), BF16),
            pltpu.VMEM((HD, 3 * T), BF16),
            pltpu.VMEM((3 * T, HD), F32),
            pltpu.VMEM((HD, QB), F32),
            pltpu.VMEM((SPAN, 2 * QB), F32),
            pltpu.VMEM((SPAN, 2 * QB), BF16),
            pltpu.VMEM((SPAN, 2 * QB), BF16),
            pltpu.VMEM((3 * T, HD), F32),
            pltpu.VMEM((3 * T, HD), F32),
            pltpu.VMEM((heads, 2, T, HD), F32),
            pltpu.VMEM((heads, 2, T, HD), BF16),
            pltpu.VMEM((heads, 2, T, HD), BF16),
            pltpu.VMEM((heads, 2, T, HD), BF16),
            pltpu.VMEM((heads, 2, T, HD), BF16),
            pltpu.VMEM((HD, QB), F32),
            pltpu.VMEM((8, HD), F32),
            pltpu.VMEM((dp_size * inner, 8, HD), F32),
            pltpu.VMEM((outer, 8, HD), F32),
            pltpu.VMEM((8, HD), F32),
            pltpu.VMEM((2, HD), F32),
            pltpu.SMEM((2, blocks), jnp.int32),
            dma((4,)),
            dma((heads, 4)),
            dma((heads, 4)),
            dma((heads, 2, 2)),
            dma((heads, 2, 2)),
            dma((heads, 2)),
            dma((heads, 2)),
            dma((heads, 2)),
            dma((heads, 2)),
            dma((heads, 2)),
            dma((heads, 2)),
            dma((exchanges,)),
            dma((exchanges,)),
        ],
        compiler_params=pltpu.CompilerParams(
            collective_id=0, has_side_effects=True, vmem_limit_bytes=VMEM_LIMIT
        ),
    )(*inputs)
    attended, query_grad, key_grad, value_grad, query_gain, key_gain = pl.pallas_call(
        flush,
        out_shape=(wide, wide, narrow, narrow, gain, gain),
        in_specs=[any_spec] * 5,
        out_specs=[any_spec] * 6,
        scratch_shapes=[dma((6,))],
        compiler_params=pltpu.CompilerParams(vmem_limit_bytes=1024 * 1024),
    )(*results)
    return (
        attended[None],
        query_grad[None],
        key_grad[None],
        value_grad[None],
        query_gain.reshape(HD),
        key_gain.reshape(HD),
    )


def solution(mesh):
    ctx_size = mesh.shape["ctx"]
    dp_size = mesh.shape["dp"]
    inner = 4 if ctx_size % 4 == 0 else 1
    row = P("dp", "ctx", None)
    return jax.shard_map(
        functools.partial(body, (ctx_size, dp_size, inner)),
        mesh=mesh,
        in_specs=(row, row, row, row, P(), P(), P("dp", None), P("dp", None)),
        out_specs=(row, row, row, row, P(), P()),
        check_vma=False,
    )
```

```python
import functools

import jax
import jax.numpy as jnp
from jax import lax
from jax.experimental import pallas as pl
from jax.experimental.pallas import tpu as pltpu
from jax.sharding import PartitionSpec as P

WINDOW = 1024
BLOCK = 1024
MESH = pl.DeviceIdType.MESH
F32 = jnp.float32
BF16 = jnp.bfloat16

score_scale = 168.0 ** (-0.5)
LOG2E = 1.4426950408889634
norm_eps = 1e-06
MASKED = -1e30

HD = 128
T = 512
QB = 256
KB = 256
SPAN = WINDOW + QB
VMEM_LIMIT = 46 * 1024 * 1024
NEAR_AHEAD = 3
FINISH_LAG = 3


def dot(a, b):
    return lax.dot_general(a, b, (((1,), (0,)), ((), ())), preferred_element_type=F32)


def fold_rows(x, op):
    return op(x.reshape(x.shape[0] // 8, 8, x.shape[1]), axis=0)


def kernel(
    heads,
    ctx_size,
    dp_size,
    inner,
    q_hbm,
    k_hbm,
    v_hbm,
    do_hbm,
    qs_hbm,
    ks_hbm,
    doc_hbm,
    end_hbm,
    att_hbm,
    dq_hbm,
    dk_hbm,
    dv_hbm,
    gains_hbm,
    qbuf,
    dobuf,
    kvbuf,
    attbuf,
    dqbuf,
    dkvout,
    kn,
    knt,
    vt,
    khat,
    qst,
    s_buf,
    p_buf,
    ds_buf,
    dkacc,
    dvacc,
    own,
    g2send,
    g1buf,
    g2recv,
    g1recv,
    qsacc,
    ksacc,
    ar1,
    ar2,
    gains,
    scales,
    docs,
    small_sem,
    load_sem,
    store_sem,
    a_send,
    a_recv,
    r_send,
    r_recv,
    g2_send,
    g2_recv,
    g1_send,
    g1_recv,
    ar_send,
    ar_recv,
):
    me = lax.axis_index("ctx")
    dp = lax.axis_index("dp")
    nxt = lax.rem(me + 1, ctx_size)
    prv = lax.rem(me + ctx_size - 1, ctx_size)
    last = heads - 1
    outer = ctx_size // inner
    me_in = lax.rem(me, inner)
    me_out = me // inner

    def load_copies(h):
        wide = pl.ds(pl.multiple_of(h * 2 * HD, 2 * HD), 2 * HD)
        narrow = pl.ds(pl.multiple_of(h * HD, HD), HD)
        return (
            pltpu.make_async_copy(k_hbm.at[:, narrow], kvbuf.at[h, 0, pl.ds(2 * T, T)], load_sem.at[h, 0]),
            pltpu.make_async_copy(v_hbm.at[:, narrow], kvbuf.at[h, 1, pl.ds(2 * T, T)], load_sem.at[h, 1]),
            pltpu.make_async_copy(q_hbm.at[:, wide], qbuf.at[h], load_sem.at[h, 2]),
            pltpu.make_async_copy(do_hbm.at[:, wide], dobuf.at[h], load_sem.at[h, 3]),
        )

    def query_stores(h):
        wide = pl.ds(pl.multiple_of(h * 2 * HD, 2 * HD), 2 * HD)
        return (
            pltpu.make_async_copy(attbuf.at[h], att_hbm.at[:, wide], store_sem.at[h, 0]),
            pltpu.make_async_copy(dqbuf.at[h], dq_hbm.at[:, wide], store_sem.at[h, 1]),
        )

    def key_stores(h):
        narrow = pl.ds(pl.multiple_of(h * HD, HD), HD)
        return (
            pltpu.make_async_copy(dkvout.at[h, 0], dk_hbm.at[:, narrow], store_sem.at[h, 2]),
            pltpu.make_async_copy(dkvout.at[h, 1], dv_hbm.at[:, narrow], store_sem.at[h, 3]),
        )

    def remote(src, dst, send, recv, device):
        return pltpu.make_async_remote_copy(
            src_ref=src, dst_ref=dst, send_sem=send, recv_sem=recv, device_id=device, device_id_type=MESH
        )

    def halo_near(h, half):
        narrow = pl.ds(pl.multiple_of(h * HD, HD), HD)
        source = pl.ds(half * QB, QB)
        place = pl.ds(T + half * QB, QB)
        return [
            remote(
                hbm.at[source, narrow],
                kvbuf.at[h, kv, place],
                a_send.at[h, half, kv],
                a_recv.at[h, half, kv],
                {"ctx": nxt},
            )
            for kv, hbm in enumerate((k_hbm, v_hbm))
        ]

    def halo_far(h, half):
        return remote(
            kvbuf.at[h, :, pl.ds(T + half * QB, QB)],
            kvbuf.at[h, :, pl.ds(half * QB, QB)],
            r_send.at[h, half],
            r_recv.at[h, half],
            {"ctx": nxt},
        )

    def grad_far(h, kv):
        return remote(g2send.at[h, kv], g2recv.at[h, kv], g2_send.at[h, kv], g2_recv.at[h, kv], {"ctx": prv})

    def grad_near(h, kv):
        return remote(g1buf.at[h, kv], g1recv.at[h, kv], g1_send.at[h, kv], g1_recv.at[h, kv], {"ctx": prv})

    def partners(stage):
        if stage == 0:
            return [
                {"dp": lax.rem(dp + d, dp_size), "ctx": me_out * inner + lax.rem(me_in + c, inner)}
                for d in range(dp_size)
                for c in range(inner)
                if d or c
            ]
        return [{"ctx": lax.rem(me_out + d, outer) * inner + me_in} for d in range(1, outer)]

    stage_slot = (dp * inner + me_in, me_out)
    stage_buf = (ar1, ar2)
    stage_base = (0, dp_size * inner - 1)

    def stage_copies(stage):
        slot = stage_buf[stage].at[stage_slot[stage]]
        base = stage_base[stage]
        return [
            remote(slot, slot, ar_send.at[base + d], ar_recv.at[base + d], device)
            for d, device in enumerate(partners(stage))
        ]

    def stage_start(stage, value):
        stage_buf[stage][stage_slot[stage]] = value
        for copy in stage_copies(stage):
            copy.start()

    def stage_sum(stage):
        for copy in stage_copies(stage):
            copy.wait()
        total = stage_buf[stage][0]
        for slot in range(1, stage_buf[stage].shape[0]):
            total = total + stage_buf[stage][slot]
        return total

    small_copies = (
        pltpu.make_async_copy(qs_hbm, scales.at[pl.ds(0, 1)], small_sem.at[0]),
        pltpu.make_async_copy(ks_hbm, scales.at[pl.ds(1, 1)], small_sem.at[1]),
        pltpu.make_async_copy(doc_hbm, docs.at[pl.ds(0, 1)], small_sem.at[2]),
        pltpu.make_async_copy(end_hbm, docs.at[pl.ds(1, 1)], small_sem.at[3]),
    )
    def start_loads(h, carry):
        for copy in load_copies(h):
            copy.start()
        return carry

    barrier = pltpu.get_barrier_semaphore()
    greeted = [{"ctx": nxt}, {"ctx": prv}] + partners(0) + partners(1)
    for device in greeted:
        pl.semaphore_signal(barrier, inc=1, device_id=device, device_id_type=MESH)
    for copy in small_copies:
        copy.start()
    start_loads(0, 0)
    pl.semaphore_wait(barrier, len(greeted))

    def start_halo(h):
        for half in (1, 0):
            for copy in halo_near(h, half):
                copy.start()

    def relay(h):
        for half in (1, 0):
            for copy in halo_near(h, half):
                copy.wait_recv()
            halo_far(h, half).start()

    start_halo(0)
    lax.fori_loop(1, heads, start_loads, 0)
    relay(0)
    for h in range(1, min(NEAR_AHEAD, heads)):
        start_halo(h)

    for copy in small_copies:
        copy.wait()
    qrow = scales[0:1, :]
    krow = scales[1:2, :]
    half = jnp.transpose(jnp.broadcast_to(qrow, (HD, HD)))
    qst[...] = jnp.concatenate([half, half], axis=1)
    qsacc[...] = jnp.zeros_like(qsacc)
    ksacc[...] = jnp.zeros_like(ksacc)

    block = me * T // BLOCK
    doc = docs[0, block]
    before = docs[0, jnp.maximum(block - 1, 0)]
    same = (block > 0) & (doc == before)
    into = me * T - block * BLOCK
    first = jnp.where(same, 0, 2 * T - into)
    limit = docs[1, doc] - (me - 2) * T

    def prepare(h, b):
        rows = slice(b * KB, (b + 1) * KB)
        x = kvbuf[h, 0, rows, :].astype(F32)
        mean_square = jnp.mean(x * x, axis=1, keepdims=True)
        hat = x * lax.rsqrt(mean_square + norm_eps)
        khat[rows, :] = hat
        normed = (hat * krow).astype(BF16)
        kn[rows, :] = normed
        knt[:, rows] = jnp.transpose(normed)
        vt[:, rows] = jnp.transpose(kvbuf[h, 1, rows, :])

    def unit(h, g, j, kept):
        rows = pl.ds(j * QB, QB)
        cols = pl.ds(g * HD, HD)
        lanes = slice(g * QB, (g + 1) * QB)
        k0 = j * QB
        nb = SPAN // KB
        blocks = [slice(b * KB, (b + 1) * KB) for b in range(nb)]
        gain = qst[...]
        xt = jnp.transpose(qbuf[h, rows, cols].astype(F32))
        mean_square = jnp.mean(xt * xt, axis=0, keepdims=True)
        r = lax.rsqrt(mean_square + norm_eps)
        qt = (xt * r * gain).astype(BF16)
        dot_t = jnp.transpose(dobuf[h, rows, cols])
        kept.append(jnp.transpose(qt))
        lane = lax.broadcasted_iota(jnp.int32, (1, QB), 1)
        low = jnp.maximum(first, k0 + 1 + lane)
        high = jnp.minimum(limit, k0 + 1 + WINDOW + lane)
        place = lax.broadcasted_iota(jnp.int32, (KB, QB), 0)
        peak = jnp.full((8, QB), MASKED, F32)
        for b in range(nb):
            s = dot(kn[k0 + b * KB : k0 + (b + 1) * KB, :], qt)
            spot = place + (k0 + b * KB)
            s = jnp.where((spot >= low) & (spot < high), s, MASKED)
            s_buf[blocks[b], lanes] = s
            peak = jnp.maximum(peak, fold_rows(s, jnp.max))
        peak = jnp.max(peak, axis=0, keepdims=True)
        yield
        total = jnp.zeros((8, QB), F32)
        for b in range(nb):
            e = jnp.exp2((s_buf[blocks[b], lanes] - peak) * (score_scale * LOG2E))
            s_buf[blocks[b], lanes] = e
            total = total + fold_rows(e, jnp.sum)
        inverse = 1.0 / jnp.sum(total, axis=0, keepdims=True)
        for b in range(nb):
            p_buf[blocks[b], lanes] = (s_buf[blocks[b], lanes] * inverse).astype(BF16)
        yield
        o = dot(vt[:, k0 : k0 + SPAN], p_buf[:, lanes]).astype(BF16)
        attbuf[h, rows, cols] = jnp.transpose(o)
        delta = jnp.sum(dot_t.astype(F32) * o.astype(F32), axis=0, keepdims=True)
        for b in range(nb):
            part = dot(kvbuf[h, 1, k0 + b * KB : k0 + (b + 1) * KB, :], dot_t)
            shares = s_buf[blocks[b], lanes] * inverse
            ds_buf[blocks[b], lanes] = (shares * (part - delta) * score_scale).astype(BF16)
        yield
        dqt = dot(knt[:, k0 : k0 + SPAN], ds_buf[:, lanes])
        gs = dqt * gain
        lean = jnp.mean(gs * xt, axis=0, keepdims=True)
        dx = gs * r - xt * (r * r * r * lean)
        dqbuf[h, rows, cols] = jnp.transpose(dx.astype(BF16))
        qsacc[...] += dqt * (xt * r)
        yield

    def unit_pair(h, j):
        rows = pl.ds(j * QB, QB)
        k0 = j * QB
        kept = []
        one, two = unit(h, 0, j, kept), unit(h, 1, j, kept)
        for stage in (one, two, one, one, two, two, one, two):
            next(stage)
        queries = jnp.concatenate(kept, axis=0)
        grads = jnp.concatenate([dobuf[h, rows, 0:HD], dobuf[h, rows, HD : 2 * HD]], axis=0)
        dv = dot(p_buf[...], grads)
        dk = dot(ds_buf[...], queries)
        if j == 1:
            dkacc[k0 : k0 + SPAN, :] = dk
            dvacc[k0 : k0 + SPAN, :] = dv
        else:
            dkacc[0:QB, :] = dk[:QB]
            dvacc[0:QB, :] = dv[:QB]
            dkacc[QB:SPAN, :] += dk[QB:]
            dvacc[QB:SPAN, :] += dv[QB:]

    def send_parts(h):
        far_k = dkacc[0:T, :].astype(BF16)
        near_k = dkacc[T : 2 * T, :].astype(BF16)
        own_k = dkacc[2 * T : 3 * T, :]
        ksacc[...] += (
            fold_rows(far_k.astype(F32) * khat[0:T, :], jnp.sum)
            + fold_rows(near_k.astype(F32) * khat[T : 2 * T, :], jnp.sum)
            + fold_rows(own_k * khat[2 * T : 3 * T, :], jnp.sum)
        )
        g2send[h, 1] = dvacc[0:T, :].astype(BF16)
        g2send[h, 0] = far_k

        @pl.when(h == last)
        def _():
            query_part = jnp.sum(jnp.transpose(qsacc[...]), axis=0, keepdims=True)
            key_part = jnp.sum(ksacc[...], axis=0, keepdims=True)
            row = lax.broadcasted_iota(jnp.int32, (8, HD), 0)
            stage_start(0, jnp.where(row == 0, query_part, jnp.where(row == 1, key_part, 0.0)))

        grad_far(h, 1).start()
        grad_far(h, 0).start()
        g1buf[h, 0] = near_k
        g1buf[h, 1] = dvacc[T : 2 * T, :].astype(BF16)
        own[h, 0] = own_k
        own[h, 1] = dvacc[2 * T : 3 * T, :]

    def merge(h):
        for kv in (1, 0):
            grad_far(h, kv).wait_recv()
            g1buf[h, kv] = (g1buf[h, kv].astype(F32) + g2recv[h, kv].astype(F32)).astype(BF16)
            grad_near(h, kv).start()

    def finish(h):
        grad_near(h, 1).wait_recv()
        dkvout[h, 1] = (own[h, 1] + g1recv[h, 1].astype(F32)).astype(BF16)
        grad_near(h, 0).wait_recv()
        total_k = own[h, 0] + g1recv[h, 0].astype(F32)
        x = kvbuf[h, 0, pl.ds(2 * T, T), :].astype(F32)
        r = lax.rsqrt(jnp.mean(x * x, axis=1, keepdims=True) + norm_eps)
        gs = total_k * krow
        lean = jnp.mean(gs * x, axis=1, keepdims=True)
        dkvout[h, 0] = (gs * r - x * (r * r * r * lean)).astype(BF16)
        for copy in key_stores(h):
            copy.start()

    def hand_on(h):
        @pl.when(h + 1 < heads)
        def _():
            relay(h + 1)

        @pl.when(h + NEAR_AHEAD < heads)
        def _():
            start_halo(h + NEAR_AHEAD)

    def step(h, carry):
        for copy in load_copies(h):
            copy.wait()
        halo_far(h, 1).wait_recv()

        @pl.when(h > 0)
        def _():
            hand_on(h)

        for b in range(1, 3 * T // KB):
            prepare(h, b)
        unit_pair(h, 1)

        @pl.when(h >= 1)
        def _():
            merge(h - 1)

        halo_far(h, 0).wait_recv()
        prepare(h, 0)
        unit_pair(h, 0)
        send_parts(h)
        for copy in query_stores(h):
            copy.start()

        @pl.when(h == 0)
        def _():
            hand_on(h)

        @pl.when(h >= FINISH_LAG)
        def _():
            finish(h - FINISH_LAG)

        return carry

    lax.fori_loop(0, heads, step, 0)

    for h in range(heads - FINISH_LAG, heads - 2):
        finish(h)
    def drain(h, carry):
        for half in range(2):
            for copy in halo_near(h, half):
                copy.wait_send()
            halo_far(h, half).wait_send()
            grad_far(h, half).wait_send()
            grad_near(h, half).wait_send()
        for copy in query_stores(h) + key_stores(h):
            copy.wait()
        return carry

    stage_start(1, stage_sum(0))
    lax.fori_loop(0, heads - 2, drain, 0)
    merge(last)
    finish(last - 1)
    gains[...] = stage_sum(1)
    gains_copy = pltpu.make_async_copy(gains, gains_hbm, small_sem.at[0])
    gains_copy.start()
    finish(last)

    lax.fori_loop(heads - 2, heads, drain, 0)
    gains_copy.wait()


def flush(*refs):
    sources, targets, sem = refs[:5], refs[5:11], refs[11]
    copies = [
        pltpu.make_async_copy(source, target, sem.at[i])
        for i, (source, target) in enumerate(zip(sources[:4], targets[:4]))
    ]
    copies.append(pltpu.make_async_copy(sources[4].at[pl.ds(0, 1)], targets[4], sem.at[4]))
    copies.append(pltpu.make_async_copy(sources[4].at[pl.ds(1, 1)], targets[5], sem.at[5]))
    for copy in copies:
        copy.start()
    for copy in copies:
        copy.wait()


def body(mesh_shape, query_raw, key_raw, values, out_grad, query_scale, key_scale, block_doc, doc_end):
    ctx_size, dp_size, inner = mesh_shape
    tokens = query_raw.shape[1]
    blocks = block_doc.shape[1]
    heads = key_raw.shape[2] // HD
    outer = ctx_size // inner
    exchanges = dp_size * inner + outer - 2
    any_spec = pl.BlockSpec(memory_space=pl.ANY)
    hbm_spec = pl.BlockSpec(memory_space=pltpu.HBM)
    dma = pltpu.SemaphoreType.DMA
    wide = jax.ShapeDtypeStruct((tokens, 2 * heads * HD), BF16)
    narrow = jax.ShapeDtypeStruct((tokens, heads * HD), BF16)
    gain = jax.ShapeDtypeStruct((1, HD), F32)
    inputs = [
        pltpu.with_memory_space_constraint(x, pltpu.HBM)
        for x in (
            query_raw[0],
            key_raw[0],
            values[0],
            out_grad[0],
            query_scale.reshape(1, HD),
            key_scale.reshape(1, HD),
            block_doc,
            doc_end,
        )
    ]
    results = pl.pallas_call(
        functools.partial(kernel, heads, ctx_size, dp_size, inner),
        out_shape=(wide, wide, narrow, narrow, jax.ShapeDtypeStruct((8, HD), F32)),
        in_specs=[hbm_spec] * 8,
        out_specs=[any_spec] * 5,
        scratch_shapes=[
            pltpu.VMEM((heads, T, 2 * HD), BF16),
            pltpu.VMEM((heads, T, 2 * HD), BF16),
            pltpu.VMEM((heads, 2, 3 * T, HD), BF16),
            pltpu.VMEM((heads, T, 2 * HD), BF16),
            pltpu.VMEM((heads, T, 2 * HD), BF16),
            pltpu.VMEM((heads, 2, T, HD), BF16),
            pltpu.VMEM((3 * T, HD), BF16),
            pltpu.VMEM((HD, 3 * T), BF16),
            pltpu.VMEM((HD, 3 * T), BF16),
            pltpu.VMEM((3 * T, HD), F32),
            pltpu.VMEM((HD, QB), F32),
            pltpu.VMEM((SPAN, 2 * QB), F32),
            pltpu.VMEM((SPAN, 2 * QB), BF16),
            pltpu.VMEM((SPAN, 2 * QB), BF16),
            pltpu.VMEM((3 * T, HD), F32),
            pltpu.VMEM((3 * T, HD), F32),
            pltpu.VMEM((heads, 2, T, HD), F32),
            pltpu.VMEM((heads, 2, T, HD), BF16),
            pltpu.VMEM((heads, 2, T, HD), BF16),
            pltpu.VMEM((heads, 2, T, HD), BF16),
            pltpu.VMEM((heads, 2, T, HD), BF16),
            pltpu.VMEM((HD, QB), F32),
            pltpu.VMEM((8, HD), F32),
            pltpu.VMEM((dp_size * inner, 8, HD), F32),
            pltpu.VMEM((outer, 8, HD), F32),
            pltpu.VMEM((8, HD), F32),
            pltpu.VMEM((2, HD), F32),
            pltpu.SMEM((2, blocks), jnp.int32),
            dma((4,)),
            dma((heads, 4)),
            dma((heads, 4)),
            dma((heads, 2, 2)),
            dma((heads, 2, 2)),
            dma((heads, 2)),
            dma((heads, 2)),
            dma((heads, 2)),
            dma((heads, 2)),
            dma((heads, 2)),
            dma((heads, 2)),
            dma((exchanges,)),
            dma((exchanges,)),
        ],
        compiler_params=pltpu.CompilerParams(
            collective_id=0, has_side_effects=True, vmem_limit_bytes=VMEM_LIMIT
        ),
    )(*inputs)
    attended, query_grad, key_grad, value_grad, query_gain, key_gain = pl.pallas_call(
        flush,
        out_shape=(wide, wide, narrow, narrow, gain, gain),
        in_specs=[any_spec] * 5,
        out_specs=[any_spec] * 6,
        scratch_shapes=[dma((6,))],
        compiler_params=pltpu.CompilerParams(vmem_limit_bytes=1024 * 1024),
    )(*results)
    return (
        attended[None],
        query_grad[None],
        key_grad[None],
        value_grad[None],
        query_gain.reshape(HD),
        key_gain.reshape(HD),
    )


def solution(mesh):
    ctx_size = mesh.shape["ctx"]
    dp_size = mesh.shape["dp"]
    inner = 4 if ctx_size % 4 == 0 else 1
    row = P("dp", "ctx", None)
    return jax.shard_map(
        functools.partial(body, (ctx_size, dp_size, inner)),
        mesh=mesh,
        in_specs=(row, row, row, row, P(), P(), P("dp", None), P("dp", None)),
        out_specs=(row, row, row, row, P(), P()),
        check_vma=False,
    )
```

```python
import functools

import jax
import jax.numpy as jnp
from jax import lax
from jax.experimental import pallas as pl
from jax.experimental.pallas import tpu as pltpu
from jax.sharding import PartitionSpec as P

WINDOW = 1024
BLOCK = 1024
MESH = pl.DeviceIdType.MESH
F32 = jnp.float32
BF16 = jnp.bfloat16

score_scale = 168.0 ** (-0.5)
LOG2E = 1.4426950408889634
norm_eps = 1e-06
MASKED = -1e30

HD = 128
T = 512
QB = 256
KB = 256
SPAN = WINDOW + QB
VMEM_LIMIT = 46 * 1024 * 1024
NEAR_AHEAD = 4
FINISH_LAG = 3


def dot(a, b):
    return lax.dot_general(a, b, (((1,), (0,)), ((), ())), preferred_element_type=F32)


def fold_rows(x, op):
    return op(x.reshape(x.shape[0] // 8, 8, x.shape[1]), axis=0)


def kernel(
    heads,
    ctx_size,
    dp_size,
    inner,
    q_hbm,
    k_hbm,
    v_hbm,
    do_hbm,
    qs_hbm,
    ks_hbm,
    doc_hbm,
    end_hbm,
    att_hbm,
    dq_hbm,
    dk_hbm,
    dv_hbm,
    gains_hbm,
    qbuf,
    dobuf,
    kvbuf,
    attbuf,
    dqbuf,
    dkvout,
    kn,
    knt,
    vt,
    khat,
    qst,
    s_buf,
    p_buf,
    ds_buf,
    dkacc,
    dvacc,
    own,
    g2send,
    g1buf,
    g2recv,
    g1recv,
    qsacc,
    ksacc,
    ar1,
    ar2,
    gains,
    scales,
    docs,
    small_sem,
    load_sem,
    store_sem,
    a_send,
    a_recv,
    r_send,
    r_recv,
    g2_send,
    g2_recv,
    g1_send,
    g1_recv,
    ar_send,
    ar_recv,
):
    me = lax.axis_index("ctx")
    dp = lax.axis_index("dp")
    nxt = lax.rem(me + 1, ctx_size)
    prv = lax.rem(me + ctx_size - 1, ctx_size)
    last = heads - 1
    outer = ctx_size // inner
    me_in = lax.rem(me, inner)
    me_out = me // inner

    def load_copies(h):
        wide = pl.ds(pl.multiple_of(h * 2 * HD, 2 * HD), 2 * HD)
        narrow = pl.ds(pl.multiple_of(h * HD, HD), HD)
        return (
            pltpu.make_async_copy(k_hbm.at[:, narrow], kvbuf.at[h, 0, pl.ds(2 * T, T)], load_sem.at[h, 0]),
            pltpu.make_async_copy(v_hbm.at[:, narrow], kvbuf.at[h, 1, pl.ds(2 * T, T)], load_sem.at[h, 1]),
            pltpu.make_async_copy(q_hbm.at[:, wide], qbuf.at[h], load_sem.at[h, 2]),
            pltpu.make_async_copy(do_hbm.at[:, wide], dobuf.at[h], load_sem.at[h, 3]),
        )

    def query_stores(h):
        wide = pl.ds(pl.multiple_of(h * 2 * HD, 2 * HD), 2 * HD)
        return (
            pltpu.make_async_copy(attbuf.at[h], att_hbm.at[:, wide], store_sem.at[h, 0]),
            pltpu.make_async_copy(dqbuf.at[h], dq_hbm.at[:, wide], store_sem.at[h, 1]),
        )

    def key_stores(h):
        narrow = pl.ds(pl.multiple_of(h * HD, HD), HD)
        return (
            pltpu.make_async_copy(dkvout.at[h, 0], dk_hbm.at[:, narrow], store_sem.at[h, 2]),
            pltpu.make_async_copy(dkvout.at[h, 1], dv_hbm.at[:, narrow], store_sem.at[h, 3]),
        )

    def remote(src, dst, send, recv, device):
        return pltpu.make_async_remote_copy(
            src_ref=src, dst_ref=dst, send_sem=send, recv_sem=recv, device_id=device, device_id_type=MESH
        )

    def halo_near(h, half):
        narrow = pl.ds(pl.multiple_of(h * HD, HD), HD)
        source = pl.ds(half * QB, QB)
        place = pl.ds(T + half * QB, QB)
        return [
            remote(
                hbm.at[source, narrow],
                kvbuf.at[h, kv, place],
                a_send.at[h, half, kv],
                a_recv.at[h, half, kv],
                {"ctx": nxt},
            )
            for kv, hbm in enumerate((k_hbm, v_hbm))
        ]

    def halo_far(h, half):
        return remote(
            kvbuf.at[h, :, pl.ds(T + half * QB, QB)],
            kvbuf.at[h, :, pl.ds(half * QB, QB)],
            r_send.at[h, half],
            r_recv.at[h, half],
            {"ctx": nxt},
        )

    def grad_far(h, kv):
        return remote(g2send.at[h, kv], g2recv.at[h, kv], g2_send.at[h, kv], g2_recv.at[h, kv], {"ctx": prv})

    def grad_near(h, kv):
        return remote(g1buf.at[h, kv], g1recv.at[h, kv], g1_send.at[h, kv], g1_recv.at[h, kv], {"ctx": prv})

    def partners(stage):
        if stage == 0:
            return [
                {"dp": lax.rem(dp + d, dp_size), "ctx": me_out * inner + lax.rem(me_in + c, inner)}
                for d in range(dp_size)
                for c in range(inner)
                if d or c
            ]
        return [{"ctx": lax.rem(me_out + d, outer) * inner + me_in} for d in range(1, outer)]

    stage_slot = (dp * inner + me_in, me_out)
    stage_buf = (ar1, ar2)
    stage_base = (0, dp_size * inner - 1)

    def stage_copies(stage):
        slot = stage_buf[stage].at[stage_slot[stage]]
        base = stage_base[stage]
        return [
            remote(slot, slot, ar_send.at[base + d], ar_recv.at[base + d], device)
            for d, device in enumerate(partners(stage))
        ]

    def stage_start(stage, value):
        stage_buf[stage][stage_slot[stage]] = value
        for copy in stage_copies(stage):
            copy.start()

    def stage_sum(stage):
        for copy in stage_copies(stage):
            copy.wait()
        total = stage_buf[stage][0]
        for slot in range(1, stage_buf[stage].shape[0]):
            total = total + stage_buf[stage][slot]
        return total

    small_copies = (
        pltpu.make_async_copy(qs_hbm, scales.at[pl.ds(0, 1)], small_sem.at[0]),
        pltpu.make_async_copy(ks_hbm, scales.at[pl.ds(1, 1)], small_sem.at[1]),
        pltpu.make_async_copy(doc_hbm, docs.at[pl.ds(0, 1)], small_sem.at[2]),
        pltpu.make_async_copy(end_hbm, docs.at[pl.ds(1, 1)], small_sem.at[3]),
    )
    def start_loads(h, carry):
        for copy in load_copies(h):
            copy.start()
        return carry

    barrier = pltpu.get_barrier_semaphore()
    greeted = [{"ctx": nxt}, {"ctx": prv}] + partners(0) + partners(1)
    for device in greeted:
        pl.semaphore_signal(barrier, inc=1, device_id=device, device_id_type=MESH)
    for copy in small_copies:
        copy.start()
    start_loads(0, 0)
    pl.semaphore_wait(barrier, len(greeted))

    def start_halo(h):
        for half in (1, 0):
            for copy in halo_near(h, half):
                copy.start()

    def relay(h):
        for half in (1, 0):
            for copy in halo_near(h, half):
                copy.wait_recv()
            halo_far(h, half).start()

    start_halo(0)
    lax.fori_loop(1, heads, start_loads, 0)
    relay(0)
    for h in range(1, min(NEAR_AHEAD, heads)):
        start_halo(h)

    for copy in small_copies:
        copy.wait()
    qrow = scales[0:1, :]
    krow = scales[1:2, :]
    half = jnp.transpose(jnp.broadcast_to(qrow, (HD, HD)))
    qst[...] = jnp.concatenate([half, half], axis=1)
    qsacc[...] = jnp.zeros_like(qsacc)
    ksacc[...] = jnp.zeros_like(ksacc)

    block = me * T // BLOCK
    doc = docs[0, block]
    before = docs[0, jnp.maximum(block - 1, 0)]
    same = (block > 0) & (doc == before)
    into = me * T - block * BLOCK
    first = jnp.where(same, 0, 2 * T - into)
    limit = docs[1, doc] - (me - 2) * T

    def prepare(h, b):
        rows = slice(b * KB, (b + 1) * KB)
        x = kvbuf[h, 0, rows, :].astype(F32)
        mean_square = jnp.mean(x * x, axis=1, keepdims=True)
        hat = x * lax.rsqrt(mean_square + norm_eps)
        khat[rows, :] = hat
        normed = (hat * krow).astype(BF16)
        kn[rows, :] = normed
        knt[:, rows] = jnp.transpose(normed)
        vt[:, rows] = jnp.transpose(kvbuf[h, 1, rows, :])

    def unit(h, g, j, kept):
        rows = pl.ds(j * QB, QB)
        cols = pl.ds(g * HD, HD)
        lanes = slice(g * QB, (g + 1) * QB)
        k0 = j * QB
        nb = SPAN // KB
        blocks = [slice(b * KB, (b + 1) * KB) for b in range(nb)]
        gain = qst[...]
        xt = jnp.transpose(qbuf[h, rows, cols].astype(F32))
        mean_square = jnp.mean(xt * xt, axis=0, keepdims=True)
        r = lax.rsqrt(mean_square + norm_eps)
        qt = (xt * r * gain).astype(BF16)
        dot_t = jnp.transpose(dobuf[h, rows, cols])
        kept.append(jnp.transpose(qt))
        lane = lax.broadcasted_iota(jnp.int32, (1, QB), 1)
        low = jnp.maximum(first, k0 + 1 + lane)
        high = jnp.minimum(limit, k0 + 1 + WINDOW + lane)
        place = lax.broadcasted_iota(jnp.int32, (KB, QB), 0)
        peak = jnp.full((8, QB), MASKED, F32)
        for b in range(nb):
            s = dot(kn[k0 + b * KB : k0 + (b + 1) * KB, :], qt)
            spot = place + (k0 + b * KB)
            s = jnp.where((spot >= low) & (spot < high), s, MASKED)
            s_buf[blocks[b], lanes] = s
            peak = jnp.maximum(peak, fold_rows(s, jnp.max))
        peak = jnp.max(peak, axis=0, keepdims=True)
        yield
        total = jnp.zeros((8, QB), F32)
        for b in range(nb):
            e = jnp.exp2((s_buf[blocks[b], lanes] - peak) * (score_scale * LOG2E))
            s_buf[blocks[b], lanes] = e
            total = total + fold_rows(e, jnp.sum)
        inverse = 1.0 / jnp.sum(total, axis=0, keepdims=True)
        for b in range(nb):
            p_buf[blocks[b], lanes] = (s_buf[blocks[b], lanes] * inverse).astype(BF16)
        yield
        o = dot(vt[:, k0 : k0 + SPAN], p_buf[:, lanes]).astype(BF16)
        attbuf[h, rows, cols] = jnp.transpose(o)
        delta = jnp.sum(dot_t.astype(F32) * o.astype(F32), axis=0, keepdims=True)
        for b in range(nb):
            part = dot(kvbuf[h, 1, k0 + b * KB : k0 + (b + 1) * KB, :], dot_t)
            shares = s_buf[blocks[b], lanes] * inverse
            ds_buf[blocks[b], lanes] = (shares * (part - delta) * score_scale).astype(BF16)
        yield
        dqt = dot(knt[:, k0 : k0 + SPAN], ds_buf[:, lanes])
        gs = dqt * gain
        lean = jnp.mean(gs * xt, axis=0, keepdims=True)
        dx = gs * r - xt * (r * r * r * lean)
        dqbuf[h, rows, cols] = jnp.transpose(dx.astype(BF16))
        qsacc[...] += dqt * (xt * r)
        yield

    def unit_pair(h, j):
        rows = pl.ds(j * QB, QB)
        k0 = j * QB
        kept = []
        one, two = unit(h, 0, j, kept), unit(h, 1, j, kept)
        for stage in (one, two, one, one, two, two, one, two):
            next(stage)
        queries = jnp.concatenate(kept, axis=0)
        grads = jnp.concatenate([dobuf[h, rows, 0:HD], dobuf[h, rows, HD : 2 * HD]], axis=0)
        dv = dot(p_buf[...], grads)
        dk = dot(ds_buf[...], queries)
        if j == 1:
            dkacc[k0 : k0 + SPAN, :] = dk
            dvacc[k0 : k0 + SPAN, :] = dv
        else:
            dkacc[0:QB, :] = dk[:QB]
            dvacc[0:QB, :] = dv[:QB]
            dkacc[QB:SPAN, :] += dk[QB:]
            dvacc[QB:SPAN, :] += dv[QB:]

    def send_parts(h):
        far_k = dkacc[0:T, :].astype(BF16)
        near_k = dkacc[T : 2 * T, :].astype(BF16)
        own_k = dkacc[2 * T : 3 * T, :]
        ksacc[...] += (
            fold_rows(far_k.astype(F32) * khat[0:T, :], jnp.sum)
            + fold_rows(near_k.astype(F32) * khat[T : 2 * T, :], jnp.sum)
            + fold_rows(own_k * khat[2 * T : 3 * T, :], jnp.sum)
        )
        g2send[h, 1] = dvacc[0:T, :].astype(BF16)
        g2send[h, 0] = far_k

        @pl.when(h == last)
        def _():
            query_part = jnp.sum(jnp.transpose(qsacc[...]), axis=0, keepdims=True)
            key_part = jnp.sum(ksacc[...], axis=0, keepdims=True)
            row = lax.broadcasted_iota(jnp.int32, (8, HD), 0)
            stage_start(0, jnp.where(row == 0, query_part, jnp.where(row == 1, key_part, 0.0)))

        grad_far(h, 1).start()
        grad_far(h, 0).start()
        g1buf[h, 0] = near_k
        g1buf[h, 1] = dvacc[T : 2 * T, :].astype(BF16)
        own[h, 0] = own_k
        own[h, 1] = dvacc[2 * T : 3 * T, :]

    def merge(h):
        for kv in (1, 0):
            grad_far(h, kv).wait_recv()
            g1buf[h, kv] = (g1buf[h, kv].astype(F32) + g2recv[h, kv].astype(F32)).astype(BF16)
            grad_near(h, kv).start()

    def finish(h):
        grad_near(h, 1).wait_recv()
        dkvout[h, 1] = (own[h, 1] + g1recv[h, 1].astype(F32)).astype(BF16)
        grad_near(h, 0).wait_recv()
        total_k = own[h, 0] + g1recv[h, 0].astype(F32)
        x = kvbuf[h, 0, pl.ds(2 * T, T), :].astype(F32)
        r = lax.rsqrt(jnp.mean(x * x, axis=1, keepdims=True) + norm_eps)
        gs = total_k * krow
        lean = jnp.mean(gs * x, axis=1, keepdims=True)
        dkvout[h, 0] = (gs * r - x * (r * r * r * lean)).astype(BF16)
        for copy in key_stores(h):
            copy.start()

    def hand_on(h):
        @pl.when(h + 1 < heads)
        def _():
            relay(h + 1)

        @pl.when(h + NEAR_AHEAD < heads)
        def _():
            start_halo(h + NEAR_AHEAD)

    def step(h, carry):
        for copy in load_copies(h):
            copy.wait()
        halo_far(h, 1).wait_recv()

        @pl.when(h > 0)
        def _():
            hand_on(h)

        for b in range(1, 3 * T // KB):
            prepare(h, b)
        unit_pair(h, 1)

        @pl.when(h >= 1)
        def _():
            merge(h - 1)

        halo_far(h, 0).wait_recv()
        prepare(h, 0)
        unit_pair(h, 0)
        send_parts(h)
        for copy in query_stores(h):
            copy.start()

        @pl.when(h == 0)
        def _():
            hand_on(h)

        @pl.when(h >= FINISH_LAG)
        def _():
            finish(h - FINISH_LAG)

        return carry

    lax.fori_loop(0, heads, step, 0)

    for h in range(heads - FINISH_LAG, heads - 2):
        finish(h)
    def drain(h, carry):
        for half in range(2):
            for copy in halo_near(h, half):
                copy.wait_send()
            halo_far(h, half).wait_send()
            grad_far(h, half).wait_send()
            grad_near(h, half).wait_send()
        for copy in query_stores(h) + key_stores(h):
            copy.wait()
        return carry

    stage_start(1, stage_sum(0))
    lax.fori_loop(0, heads - 2, drain, 0)
    merge(last)
    finish(last - 1)
    gains[...] = stage_sum(1)
    gains_copy = pltpu.make_async_copy(gains, gains_hbm, small_sem.at[0])
    gains_copy.start()
    finish(last)

    lax.fori_loop(heads - 2, heads, drain, 0)
    gains_copy.wait()


def flush(*refs):
    sources, targets, sem = refs[:5], refs[5:11], refs[11]
    copies = [
        pltpu.make_async_copy(source, target, sem.at[i])
        for i, (source, target) in enumerate(zip(sources[:4], targets[:4]))
    ]
    copies.append(pltpu.make_async_copy(sources[4].at[pl.ds(0, 1)], targets[4], sem.at[4]))
    copies.append(pltpu.make_async_copy(sources[4].at[pl.ds(1, 1)], targets[5], sem.at[5]))
    for copy in copies:
        copy.start()
    for copy in copies:
        copy.wait()


def body(mesh_shape, query_raw, key_raw, values, out_grad, query_scale, key_scale, block_doc, doc_end):
    ctx_size, dp_size, inner = mesh_shape
    tokens = query_raw.shape[1]
    blocks = block_doc.shape[1]
    heads = key_raw.shape[2] // HD
    outer = ctx_size // inner
    exchanges = dp_size * inner + outer - 2
    any_spec = pl.BlockSpec(memory_space=pl.ANY)
    hbm_spec = pl.BlockSpec(memory_space=pltpu.HBM)
    dma = pltpu.SemaphoreType.DMA
    wide = jax.ShapeDtypeStruct((tokens, 2 * heads * HD), BF16)
    narrow = jax.ShapeDtypeStruct((tokens, heads * HD), BF16)
    gain = jax.ShapeDtypeStruct((1, HD), F32)
    inputs = [
        pltpu.with_memory_space_constraint(x, pltpu.HBM)
        for x in (
            query_raw[0],
            key_raw[0],
            values[0],
            out_grad[0],
            query_scale.reshape(1, HD),
            key_scale.reshape(1, HD),
            block_doc,
            doc_end,
        )
    ]
    results = pl.pallas_call(
        functools.partial(kernel, heads, ctx_size, dp_size, inner),
        out_shape=(wide, wide, narrow, narrow, jax.ShapeDtypeStruct((8, HD), F32)),
        in_specs=[hbm_spec] * 8,
        out_specs=[any_spec] * 5,
        scratch_shapes=[
            pltpu.VMEM((heads, T, 2 * HD), BF16),
            pltpu.VMEM((heads, T, 2 * HD), BF16),
            pltpu.VMEM((heads, 2, 3 * T, HD), BF16),
            pltpu.VMEM((heads, T, 2 * HD), BF16),
            pltpu.VMEM((heads, T, 2 * HD), BF16),
            pltpu.VMEM((heads, 2, T, HD), BF16),
            pltpu.VMEM((3 * T, HD), BF16),
            pltpu.VMEM((HD, 3 * T), BF16),
            pltpu.VMEM((HD, 3 * T), BF16),
            pltpu.VMEM((3 * T, HD), F32),
            pltpu.VMEM((HD, QB), F32),
            pltpu.VMEM((SPAN, 2 * QB), F32),
            pltpu.VMEM((SPAN, 2 * QB), BF16),
            pltpu.VMEM((SPAN, 2 * QB), BF16),
            pltpu.VMEM((3 * T, HD), F32),
            pltpu.VMEM((3 * T, HD), F32),
            pltpu.VMEM((heads, 2, T, HD), F32),
            pltpu.VMEM((heads, 2, T, HD), BF16),
            pltpu.VMEM((heads, 2, T, HD), BF16),
            pltpu.VMEM((heads, 2, T, HD), BF16),
            pltpu.VMEM((heads, 2, T, HD), BF16),
            pltpu.VMEM((HD, QB), F32),
            pltpu.VMEM((8, HD), F32),
            pltpu.VMEM((dp_size * inner, 8, HD), F32),
            pltpu.VMEM((outer, 8, HD), F32),
            pltpu.VMEM((8, HD), F32),
            pltpu.VMEM((2, HD), F32),
            pltpu.SMEM((2, blocks), jnp.int32),
            dma((4,)),
            dma((heads, 4)),
            dma((heads, 4)),
            dma((heads, 2, 2)),
            dma((heads, 2, 2)),
            dma((heads, 2)),
            dma((heads, 2)),
            dma((heads, 2)),
            dma((heads, 2)),
            dma((heads, 2)),
            dma((heads, 2)),
            dma((exchanges,)),
            dma((exchanges,)),
        ],
        compiler_params=pltpu.CompilerParams(
            collective_id=0, has_side_effects=True, vmem_limit_bytes=VMEM_LIMIT
        ),
    )(*inputs)
    attended, query_grad, key_grad, value_grad, query_gain, key_gain = pl.pallas_call(
        flush,
        out_shape=(wide, wide, narrow, narrow, gain, gain),
        in_specs=[any_spec] * 5,
        out_specs=[any_spec] * 6,
        scratch_shapes=[dma((6,))],
        compiler_params=pltpu.CompilerParams(vmem_limit_bytes=1024 * 1024),
    )(*results)
    return (
        attended[None],
        query_grad[None],
        key_grad[None],
        value_grad[None],
        query_gain.reshape(HD),
        key_gain.reshape(HD),
    )


def solution(mesh):
    ctx_size = mesh.shape["ctx"]
    dp_size = mesh.shape["dp"]
    inner = 4 if ctx_size % 4 == 0 else 1
    row = P("dp", "ctx", None)
    return jax.shard_map(
        functools.partial(body, (ctx_size, dp_size, inner)),
        mesh=mesh,
        in_specs=(row, row, row, row, P(), P(), P("dp", None), P("dp", None)),
        out_specs=(row, row, row, row, P(), P()),
        check_vma=False,
    )
```
